256 devices in a mesh: row: 8 (over y, x_hi), col: 8 (over z), rep: 4 (over x_lo, core).
Axes of the slice: x: 4 (x_hi: 2, x_lo: 2; x = x_hi * 2 + x_lo), y: 4, z: 8, core: 2. Of those that a mesh axis runs over, the one named last changes fastest.
Arguments:
- hidden: bfloat16 [2048, 28672], P('rep', 'col'), may hold values from -0.13183594 to 0.13183594
- grad_out: bfloat16 [2048, 8192], P('rep', 'row'), may hold values from -6 to 6
- weight: bfloat16 [28672, 8192], P('col', ('row', 'rep')), may hold values from -0.03125 to 0.03125
Outputs:
- grad_hidden: bfloat16 [2048, 28672], P('rep', 'col')
- grad_weight: bfloat16 [28672, 8192], P('col', ('row', 'rep'))
- left_stats: float32 [56, 512, 512], P('col', ('row', 'rep'))
- right_stats: float32 [8192, 512], P(('row', 'rep'), 'col')
The draws below stay inside these ranges and needn't reach their ends.
All inputs are finite; a program needn't handle non-finite values.
Results may differ from the reference program's by a relative error of at most 0.017.
Values may be sent and summed in bfloat16 or wider, within the bound.
No kernel may reach another device: no remote copies, remote signals or barrier semaphores. Data moves between devices by JAX's collectives and lax.ppermute only.
A program may use at most 128 MiB of HBM per device.

```python
import jax
import jax.numpy as jnp
from jax import lax

D = 8192
FF = 28672
BLK = 512
TOKENS = 2048
N_ROW = 8
N_REP = 4


def block_scale(rng, shape, split, low, top_value):
    loudness, own = 1.0, jax.random.fold_in(rng, 6)
    for axis_at, shards_of in split:
        heights = jnp.exp(jax.random.uniform(jax.random.fold_in(own, axis_at), (shards_of,), jnp.float32, low / len(split), top_value / len(split)))
        loudness = loudness * jnp.repeat(heights, shape[axis_at] // shards_of).reshape([-1 if axis == axis_at else 1 for axis in range(len(shape))])
    return loudness


def scatter_about(stream_key, shape, spread, limit, shards=(), held_as=jnp.bfloat16):
    factor_of = block_scale(stream_key, shape, shards, -0.22, 0.18) if shards else 1.0
    result = jax.random.normal(stream_key, shape, jnp.float32) * spread * factor_of
    return jnp.minimum(jnp.maximum(result, -limit), limit).astype(held_as)


def setup_inputs(seed: int = 0) -> dict:
    key_list = jax.random.split(jax.random.key(seed), 4)
    hidden = scatter_about(key_list[0], (TOKENS, FF), (TOKENS ** -0.5), 0.13183594, ((0, 4), (1, 8)))
    grad_out = scatter_about(key_list[1], (TOKENS, D), 1.0, 6.0, ((0, 4), (1, 8)))
    weight = scatter_about(key_list[2], (FF, D), FF ** -0.5, 0.03125, ((0, 8), (1, 32)))
    return {"hidden": hidden, "grad_out": grad_out, "weight": weight}


def reference(hidden, grad_out, weight):
    per_replica = hidden.shape[0] // N_REP
    weight_grad = jnp.zeros(weight.shape, jnp.float32)
    for replica in range(N_REP):
        lower = replica * per_replica
        replica_part = jnp.dot(hidden[lower:lower + per_replica].T, grad_out[lower:lower + per_replica], preferred_element_type=jnp.float32).astype(jnp.bfloat16)
        replica_part = lax.optimization_barrier(replica_part)
        weight_grad = weight_grad + replica_part.astype(jnp.float32)
    grad_weight = weight_grad.astype(jnp.bfloat16)
    row_width = D // N_ROW
    input_grad = jnp.zeros(hidden.shape, jnp.float32)
    for row_index in range(N_ROW):
        lower = row_index * row_width
        width_part = jnp.dot(grad_out[:, lower:lower + row_width], weight[:, lower:lower + row_width].T, preferred_element_type=jnp.float32).astype(jnp.bfloat16)
        width_part = lax.optimization_barrier(width_part)
        input_grad = input_grad + width_part.astype(jnp.float32)
    grad_hidden = input_grad.astype(jnp.bfloat16)
    grad_float = grad_weight.astype(jnp.float32)
    left_blocks = grad_float.reshape(FF // BLK, BLK, D)
    left_stats = jnp.einsum("abd,acd->abc", left_blocks, left_blocks, precision=lax.Precision.HIGHEST) / D
    right_blocks = grad_float.reshape(FF, D // BLK, BLK)
    right_stats = jnp.einsum("fkb,fkc->kbc", right_blocks, right_blocks, precision=lax.Precision.HIGHEST) / FF
    return grad_hidden, grad_weight, left_stats, right_stats.reshape(D, BLK)
```

```python
import jax
import jax.numpy as jnp
from jax import lax
from jax.experimental import pallas as pl
from jax.experimental.pallas import tpu as pltpu
from jax.sharding import PartitionSpec as P

D = 8192
FF = 28672
BLK = 512
N_Y = 4
A_CHUNKS = 2
GATHERED_ROWS = 1280
TILE = 256
F32 = jnp.float32
BF16 = jnp.bfloat16

Y, SECOND, FIRST, FAR, SLAB, SLAB_C, SLAB_X, SLAB_XC, CORE_AT, X_LO_AT = range(10)


def plane_perm(move):
    pairs = []
    for at in range(32):
        y, x_hi, x_lo, core = at // 8, at // 4 % 2, at // 2 % 2, at % 2
        y, x_hi, x_lo, core = move(y, x_hi, x_lo, core)
        pairs.append((at, y * 8 + x_hi * 4 + x_lo * 2 + core))
    return pairs


CORE = plane_perm(lambda y, h, l, c: (y, h, l, 1 - c))
X_LO = plane_perm(lambda y, h, l, c: (y, h, 1 - l, c))
X_HI = plane_perm(lambda y, h, l, c: (y, 1 - h, l, c))
X_OUT = plane_perm(lambda y, h, l, c: (y, 1 - h, 1 - l, c))
X_OUT_CORE = plane_perm(lambda y, h, l, c: (y, 1 - h, 1 - l, 1 - c))
Y_FIRST = plane_perm(lambda y, h, l, c: (y ^ (3 if c else 1), h, l, c))
Y_SECOND = plane_perm(lambda y, h, l, c: (y ^ (1 if c else 3), h, l, c))


def send(x, perm):
    return lax.ppermute(x, ("row", "rep"), perm)


def shape(dims, dtype=BF16):
    return jax.ShapeDtypeStruct(dims, dtype)


ANY = pl.BlockSpec(memory_space=pl.ANY)


def call(kernel, at, arrays, in_specs, outs, out_specs, grid=(1,), scratch=(), after=(), aliases=None, vmem=12, cost=1):
    n, m = len(arrays), len(after)

    def run(at_ref, *refs):
        kernel(at_ref, *refs[:n], *refs[n + m:])

    return pl.pallas_call(
        run,
        grid_spec=pltpu.PrefetchScalarGridSpec(
            num_scalar_prefetch=1,
            grid=grid,
            in_specs=list(in_specs) + [ANY] * m,
            out_specs=list(out_specs),
            scratch_shapes=list(scratch),
        ),
        out_shape=list(outs),
        input_output_aliases=aliases or {},
        compiler_params=pltpu.CompilerParams(vmem_limit_bytes=vmem * 2**20),
        cost_estimate=pl.CostEstimate(flops=1, bytes_accessed=cost, transcendentals=0),
    )(at, *arrays, *after)


def copies(at, arrays, outs, plan, count, after=()):
    n = len(arrays)

    def kernel(at_ref, *refs):
        sems = refs[-1]
        moves = [
            pltpu.make_async_copy(src, dst, sems.at[i])
            for i, (src, dst) in enumerate(plan(at_ref, refs[:n], refs[n:-1]))
        ]
        for move in moves:
            move.start()
        for move in moves:
            move.wait()

    return call(
        kernel, at, arrays, [pl.BlockSpec(memory_space=pltpu.HBM)] * n, outs,
        [pl.BlockSpec(out.shape, lambda i, at: (0, 0)) for out in outs],
        scratch=[pltpu.SemaphoreType.DMA((count,))], after=after, vmem=58,
    )


def add(at, arrays, after=()):
    rows, width = arrays[0].shape
    spec = pl.BlockSpec((rows, width // 2), lambda i, at: (0, i))

    def kernel(at_ref, *refs):
        total = refs[0][...].astype(F32)
        for ref in refs[1:-1]:
            total = total + ref[...].astype(F32)
        refs[-1][...] = total.astype(BF16)

    return call(kernel, at, arrays, [spec] * len(arrays), [shape((rows, width))], [spec], (2,), after=after)[0]


def copy_of(at, x, rows=None, after=()):
    rows = rows or x.shape[0]
    spec = pl.BlockSpec((rows // 2, x.shape[1]), lambda i, at: (i, 0))

    def kernel(at_ref, x_ref, out_ref):
        out_ref[...] = x_ref[...]

    return call(kernel, at, [x], [spec], [shape((rows, x.shape[1]))], [spec], (2,), after=after)[0]


def dot(a, b, over_a, over_b):
    return lax.dot_general(a, b, (((over_a,), (over_b,)), ((), ())), preferred_element_type=F32)


def piece(x, at, axis):
    return lax.dynamic_index_in_dim(x, at, axis, keepdims=False)


def body(hidden, grad_out, weight):
    row, rep = lax.axis_index("row"), lax.axis_index("rep")
    y, x_hi = row // 2, row % 2
    x_lo, core = rep // 2, rep % 2
    first = y ^ (1 + 2 * core)
    second = y ^ (3 - 2 * core)
    at = jnp.stack([y, second, first, y ^ 2, rep, rep ^ 1, rep ^ 2, rep ^ 3, core, x_lo]).astype(jnp.int32)
    tokens, tile_rows = hidden.shape
    slab = weight.shape[1]
    half = tile_rows // 2
    pair = 2 * slab
    n = GATHERED_ROWS
    rest = half - n
    chunk = tile_rows // A_CHUNKS
    quarter = tokens // N_Y
    half_tiles, n_tiles, chunk_tiles = half // TILE, n // TILE, chunk // TILE

    hidden_from = grad_out.shape[1]
    weight_from = hidden_from + half
    weight_blocks = tile_rows // tokens

    def pack_plan(at, ins, outs):
        other = pl.multiple_of((1 - at[CORE_AT]) * half, TILE)
        moves = [
            (ins[0], outs[0].at[:, pl.ds(0, hidden_from)]),
            (ins[1].at[:, pl.ds(other, half)], outs[0].at[:, pl.ds(hidden_from, half)]),
        ]
        for i in range(weight_blocks):
            columns = pl.ds(weight_from + i * slab, slab)
            moves.append((ins[2].at[pl.ds(i * tokens, tokens)], outs[0].at[:, columns]))
        return moves

    def hidden_plan(at, ins, outs):
        sides = [pl.multiple_of(c * half, TILE) for c in (at[CORE_AT], 1 - at[CORE_AT])]
        return [
            (ins[0].at[:, pl.ds(sides[i // 2] + starts[i % 2], parts[i % 2])], outs[i]) for i in range(4)
        ]

    cuts = [(0, 0, 2 * TILE), (0, 2 * TILE, n - 2 * TILE), (1, 0, n - 2 * TILE), (1, n - 2 * TILE, 2 * TILE)]

    def hidden_cut(at, hidden_ref, i):
        side, start, size = cuts[i]
        start = pl.multiple_of((at[CORE_AT] if side == 0 else 1 - at[CORE_AT]) * half, TILE) + start
        return hidden_ref.at[:, pl.ds(start, size)]

    cut_shapes = [shape((tokens, size)) for _, _, size in cuts]
    weight_first, hidden_first = copies(
        at, [hidden, weight], [shape((chunk, slab)), cut_shapes[0]],
        lambda at, ins, outs: [(ins[1].at[pl.ds(0, chunk)], outs[0]), (hidden_cut(at, ins[0], 0), outs[1])], 2,
    )

    def late_plan(at, ins, outs):
        moves = [(hidden_cut(at, ins[1], i), outs[i - 1]) for i in (1, 2, 3)]
        moves.append((ins[2].at[pl.ds(chunk, chunk)], outs[3]))
        return moves + pack_plan(at, ins, outs[4:])

    *hidden_late, weight_late, packed = copies(
        at, [grad_out, hidden, weight],
        cut_shapes[1:] + [shape((chunk, slab)), shape((tokens, weight_from + half))],
        late_plan, 6 + weight_blocks, after=[weight_first],
    )
    weight_x = [send(weight_first, X_LO), send(weight_late, X_LO)]
    hidden_x = [
        send(h, p) for h, p in zip([hidden_first, *hidden_late], (X_OUT, X_OUT, X_OUT_CORE, X_OUT_CORE))
    ]
    pack = send(packed, CORE)

    def turn_plan(at, ins, outs):
        moves = []
        for i, p in enumerate((Y, SECOND, FIRST, FAR)):
            for j, s in enumerate((SLAB, SLAB_C, SLAB_X, SLAB_XC)):
                src = ins[0].at[
                    pl.ds(pl.multiple_of(at[p] * quarter, quarter), quarter),
                    pl.ds(pl.multiple_of(at[s] * slab, slab), slab),
                ]
                moves.append((src, outs[0].at[pl.ds(i * quarter, quarter), pl.ds(j * slab, slab)]))
        return moves

    turned = copies(at, [grad_out], [shape(grad_out.shape)], turn_plan, 16, after=[packed])[0]

    def sum_kernel(at, hidden_ref, hidden_c_ref, out_ref, out_c_ref, result_ref):
        result_ref[...] = dot(hidden_ref[...], out_ref[...], 0, 0) + dot(hidden_c_ref[...], out_c_ref[...], 0, 0)

    tile_spec = pl.BlockSpec((TILE, pair), lambda i, at: (i, 0))
    own_columns = pl.BlockSpec((tokens, pair), lambda i, at: (0, at[X_LO_AT]))
    own_sum = call(
        sum_kernel, at, [hidden, pack, grad_out, pack],
        [
            pl.BlockSpec((tokens, TILE), lambda i, at: (0, at[CORE_AT] * half_tiles + i)),
            pl.BlockSpec((tokens, TILE), lambda i, at: (0, hidden_from // TILE + i)),
            own_columns, own_columns,
        ],
        [shape((half, pair), F32)], [tile_spec], (half_tiles,), after=[turned],
    )[0]

    lead = tokens // TILE

    def away_kernel(at, hidden_ref, hidden_c_ref, out_ref, out_c_ref, result_ref):
        i = pl.program_id(0)

        @pl.when(i < lead)
        def _():
            result_ref[...] = out_ref[pl.ds(pl.multiple_of(i * TILE, TILE), TILE)]

        @pl.when(i >= lead)
        def _():
            total = dot(hidden_ref[...], out_ref[...], 0, 0) + dot(hidden_c_ref[...], out_c_ref[...], 0, 0)
            result_ref[...] = total.astype(BF16)

    def send_away(after):
        columns = pl.BlockSpec((tokens, pair), lambda i, at: (0, 1 - at[X_LO_AT]))
        tile = lambda i: n_tiles + jnp.maximum(i - lead, 0)
        away = call(
            away_kernel, at, [hidden, pack, grad_out, pack],
            [
                pl.BlockSpec((tokens, TILE), lambda i, at: (0, at[CORE_AT] * half_tiles + tile(i))),
                pl.BlockSpec((tokens, TILE), lambda i, at: (0, hidden_from // TILE + tile(i))),
                columns, columns,
            ],
            [shape((tokens + rest, pair))], [tile_spec], (lead + rest // TILE,), after=after,
        )[0]
        return away, send(away, X_LO)

    def width_kernel(at, turned_ref, *refs):
        total = 0.0
        for j in range(4):
            total = total + dot(turned_ref[:, j * slab:(j + 1) * slab], refs[j][...], 1, 1)
        for i in range(N_Y):
            refs[4 + i][...] = total[i * quarter:(i + 1) * quarter].astype(BF16)

    def scatter_sends(own, near, off, opposite):
        return own, near, send(opposite, Y_FIRST), send(off, Y_FIRST)

    last = own_sum
    mine = []
    for k in range(A_CHUNKS):
        whole = pl.BlockSpec((TILE, slab), lambda i, at, k=k: (k * chunk_tiles + i, 0))
        chunked = pl.BlockSpec((TILE, slab), lambda i, at: (i, 0))
        per_block = tokens // TILE
        packed_spec = pl.BlockSpec(
            (TILE, slab),
            lambda i, at, k=k: ((k * chunk_tiles + i) % per_block, weight_from // slab + (k * chunk_tiles + i) // per_block),
        )
        if k == 0:
            forward = copy_of(at, weight_x[0], after=[last, hidden_x[0]])
        if k == 1:
            last, came = send_away([last, forward])
        parts = call(
            width_kernel, at, [turned, weight, pack, weight_x[k], send(forward, CORE)],
            [pl.BlockSpec(turned.shape, lambda i, at: (0, 0)), whole, packed_spec, chunked, chunked],
            [shape((quarter, chunk))] * N_Y,
            [pl.BlockSpec((quarter, TILE), lambda i, at: (0, i))] * N_Y,
            (chunk_tiles,), after=[last],
        )
        own, near, came_near, came_own = scatter_sends(*parts)
        near = add(at, [near, came_near], after=[hidden_x[1]] if k == 0 else ())
        if k == 0:
            forward = copy_of(at, weight_x[1], after=[near])
            after = [forward]
        else:
            out_came = copy_of(at, came, tokens, after=[near, hidden_x[2]])
            after = [out_came]
        last = add(at, [own, came_own, send(near, Y_SECOND)], after=after)
        mine.append(last)
    beside = [send(m, X_HI) for m in mine]
    out_xc = send(out_came, CORE)

    def grad_kernel(at, sum_ref, a_low, a_high, b_low, b_high, out_x_ref, out_xc_ref, came_ref, result_ref):
        i = pl.program_id(0)

        def gathered(a_ref, b_ref):
            total = sum_ref[...] + dot(a_ref[...], out_x_ref[...], 0, 0)
            result_ref[...] = (total + dot(b_ref[...], out_xc_ref[...], 0, 0)).astype(BF16)

        splits = [cuts[1][1] // TILE, cuts[3][1] // TILE, n_tiles]
        low = 0
        for high, refs in zip(splits, ((a_low, b_low), (a_high, b_low), (a_high, b_high))):

            @pl.when((i >= low) & (i < high))
            def _():
                gathered(*refs)

            low = high

        @pl.when(i >= n_tiles)
        def _():
            result_ref[...] = (sum_ref[...] + came_ref[...].astype(F32)).astype(BF16)

    def cut_spec(start, size):
        return pl.BlockSpec(
            (tokens, TILE), lambda i, at: (0, jnp.clip(i - start // TILE, 0, size // TILE - 1))
        )

    all_out = pl.BlockSpec((tokens, pair), lambda i, at: (0, 0))
    own_half = call(
        grad_kernel, at, [own_sum, *hidden_x, came, out_xc, came],
        [
            tile_spec, *[cut_spec(start, size) for _, start, size in cuts], all_out, all_out,
            pl.BlockSpec((TILE, pair), lambda i, at: (lead + jnp.maximum(i - n_tiles, 0), 0)),
        ],
        [shape((half, pair))], [tile_spec], (half_tiles,), after=[last, beside[0]],
    )[0]
    other_half = send(own_half, CORE)

    def right_kernel(at, own_ref, other_ref, own_slab_ref, other_slab_ref, result_ref, total_ref):
        i = pl.program_id(0)
        value = dot(own_ref[...], own_slab_ref[...], 0, 0) + dot(other_ref[...], other_slab_ref[...], 0, 0)

        @pl.when(i == 0)
        def _():
            total_ref[...] = value

        @pl.when(i > 0)
        def _():
            total_ref[...] += value

        @pl.when(i == pl.num_programs(0) - 1)
        def _():
            result_ref[...] = (total_ref[...] / FF).astype(BF16)

    steps = 2
    rows_spec = pl.BlockSpec((half // steps, pair), lambda i, at: (i, 0))
    slab_spec = pl.BlockSpec((half // steps, slab), lambda i, at: (i, at[CORE_AT]))
    right_partial = call(
        right_kernel, at, [own_half, other_half, own_half, other_half],
        [rows_spec, rows_spec, slab_spec, slab_spec],
        [shape((pair, slab))], [pl.BlockSpec((pair, slab), lambda i, at: (0, 0))], (steps,),
        scratch=[pltpu.VMEM((pair, slab), F32)],
    )[0]
    z = lax.axis_index("col")
    cols = lax.axis_size("col")
    bits = [1 << i for i in range(cols.bit_length() - 1)]
    right = right_partial.reshape([2] * len(bits) + [pair // cols, slab])
    for i, bit in enumerate(bits):
        here = z // bit % 2
        axis = len(bits) - 1 - i
        came_z = lax.ppermute(
            piece(right, 1 - here, axis).astype(BF16), "col", [(j, j ^ bit) for j in range(cols)]
        )
        right = piece(right, here, axis)
        if i < len(bits) - 1:
            right = right.astype(F32) + came_z.astype(F32)

    def last_kernel(at, mine_ref, came_ref, result_ref):
        result_ref[...] = mine_ref[...].astype(F32) + came_ref[...].astype(F32)

    spec = pl.BlockSpec(right.shape, lambda i, at: (0, 0))
    right_stats = call(
        last_kernel, at, [right, came_z], [spec] * 2, [shape(right.shape, F32)], [spec],
    )[0].T

    num = tile_rows // BLK
    mine_rows = BLK // 2 // N_Y

    def left_kernel(at, own_low, own_high, other_low, other_high, *refs):
        outs, block, product = refs[:N_Y], refs[N_Y], refs[N_Y + 1]
        a = pl.program_id(0)
        for part, own_ref, other_ref in ((0, own_low, other_low), (1, own_high, other_high)):
            held = (2 * a + part) // half_tiles == at[CORE_AT]
            block[part * TILE:(part + 1) * TILE] = jnp.where(held, own_ref[...], other_ref[...])
        groups = block[...].reshape(16, 2, 16, pair)
        my_rows = jnp.where(at[CORE_AT] == 0, groups[:, 0], groups[:, 1]).reshape(BLK // 2, pair)
        product[...] = (dot(my_rows, block[...], 1, 1) / D).astype(BF16)
        for i, p in enumerate((Y, SECOND, FIRST, FAR)):
            outs[i][0] = product[pl.ds(pl.multiple_of(at[p] * mine_rows, mine_rows), mine_rows)]

    halves = [
        pl.BlockSpec((TILE, pair), lambda a, at, part=part: ((2 * a + part) % half_tiles, 0)) for part in (0, 1)
    ]
    left = left_parts = call(
        left_kernel, at, [own_half, own_half, other_half, other_half], halves + halves,
        [shape((num, mine_rows, BLK))] * N_Y,
        [pl.BlockSpec((1, mine_rows, BLK), lambda a, at: (a, 0, 0))] * N_Y,
        (num,), scratch=[pltpu.VMEM((BLK, pair), BF16), pltpu.VMEM((BLK // 2, BLK), BF16)],
        after=[right_partial, beside[1]],
    )
    own, near, came_near, came_own = scatter_sends(*left)
    near = (near.astype(F32) + came_near.astype(F32)).astype(BF16)
    left = own.astype(F32) + came_own.astype(F32) + send(near, Y_SECOND).astype(F32)
    left = left.reshape(num, 2, 2, 16, BLK)
    sent = send(piece(left, 1 - x_lo, 2).astype(BF16), X_LO)
    left = piece(left, x_lo, 2) + sent.astype(F32)
    sent = send(piece(left, 1 - x_hi, 1).astype(BF16), X_HI)
    left_stats = piece(left, x_hi, 1) + sent.astype(F32)

    def slab_kernel(at, own_ref, other_ref, result_ref):
        held = pl.program_id(0) == at[CORE_AT]
        result_ref[...] = jnp.where(held, own_ref[...], other_ref[...])

    slab_half = pl.BlockSpec((half, slab), lambda i, at: (0, at[CORE_AT]))
    grad_slab = call(
        slab_kernel, at, [own_half, other_half], [slab_half] * 2, [shape(weight.shape)],
        [pl.BlockSpec((half, slab), lambda i, at: (i, 0))], (2,), after=left_parts[:1],
    )[0]

    def place_kernel(at, *refs):
        for j in range(N_Y):

            @pl.when(pl.program_id(0) == j)
            def _():
                refs[-1][...] = refs[j][...]

    grad_hidden = None
    for k in range(A_CHUNKS):
        total = add(at, [mine[k], beside[k]], after=[grad_slab] if k > 0 else ())
        near = send(total, Y_SECOND)
        off = send(total, Y_FIRST)
        opposite = send(near, Y_FIRST)
        given, after = [total, near, off, opposite], []
        specs = [pl.BlockSpec(total.shape, lambda i, at: (0, 0))] * N_Y
        if k > 0:
            given, specs = given + [grad_hidden], specs + [ANY]
            after = [left_stats, right_stats]
        grad_hidden = call(
            place_kernel, at, given, specs, [shape(hidden.shape)],
            [pl.BlockSpec(total.shape, lambda i, at, k=k: (at[Y + i], k))], (N_Y,),
            aliases={N_Y + 1: 0} if k > 0 else None, after=after,
        )[0]
    return grad_hidden, grad_slab, left_stats, right_stats


def solution(mesh):
    return jax.shard_map(
        body,
        mesh=mesh,
        in_specs=(P("rep", "col"), P("rep", "row"), P("col", ("row", "rep"))),
        out_specs=(
            P("rep", "col"),
            P("col", ("row", "rep")),
            P("col", ("row", "rep"), None),
            P(("row", "rep"), "col"),
        ),
        check_vma=False,
    )
```

```python
import jax
import jax.numpy as jnp
from jax import lax
from jax.experimental import pallas as pl
from jax.experimental.pallas import tpu as pltpu
from jax.sharding import PartitionSpec as P

D = 8192
FF = 28672
BLK = 512
N_Y = 4
A_CHUNKS = 2
GATHERED_ROWS = 1280
TILE = 256
F32 = jnp.float32
BF16 = jnp.bfloat16

Y, SECOND, FIRST, FAR, SLAB, SLAB_C, SLAB_X, SLAB_XC, CORE_AT, X_LO_AT, X_HI_AT, Z_HIGH = range(12)


def plane_perm(move):
    pairs = []
    for at in range(32):
        y, x_hi, x_lo, core = at // 8, at // 4 % 2, at // 2 % 2, at % 2
        y, x_hi, x_lo, core = move(y, x_hi, x_lo, core)
        pairs.append((at, y * 8 + x_hi * 4 + x_lo * 2 + core))
    return pairs


CORE = plane_perm(lambda y, h, l, c: (y, h, l, 1 - c))
X_LO = plane_perm(lambda y, h, l, c: (y, h, 1 - l, c))
X_HI = plane_perm(lambda y, h, l, c: (y, 1 - h, l, c))
X_OUT = plane_perm(lambda y, h, l, c: (y, 1 - h, 1 - l, c))
X_OUT_CORE = plane_perm(lambda y, h, l, c: (y, 1 - h, 1 - l, 1 - c))
Y_FIRST = plane_perm(lambda y, h, l, c: (y ^ (3 if c else 1), h, l, c))
Y_SECOND = plane_perm(lambda y, h, l, c: (y ^ (1 if c else 3), h, l, c))


def send(x, perm):
    return lax.ppermute(x, ("row", "rep"), perm)


def shape(dims, dtype=BF16):
    return jax.ShapeDtypeStruct(dims, dtype)


ANY = pl.BlockSpec(memory_space=pl.ANY)


def call(kernel, at, arrays, in_specs, outs, out_specs, grid=(1,), scratch=(), after=(), aliases=None, vmem=10):
    n, m = len(arrays), len(after)

    def run(at_ref, *refs):
        kernel(at_ref, *refs[:n], *refs[n + m:])

    return pl.pallas_call(
        run,
        grid_spec=pltpu.PrefetchScalarGridSpec(
            num_scalar_prefetch=1,
            grid=grid,
            in_specs=list(in_specs) + [ANY] * m,
            out_specs=list(out_specs),
            scratch_shapes=list(scratch),
        ),
        out_shape=list(outs),
        input_output_aliases=aliases or {},
        compiler_params=pltpu.CompilerParams(vmem_limit_bytes=vmem * 2**20),
        cost_estimate=pl.CostEstimate(flops=1, bytes_accessed=1, transcendentals=0),
    )(at, *arrays, *after)


def copies(at, arrays, outs, plan, count, after=(), vmem=16):
    n = len(arrays)

    def kernel(at_ref, *refs):
        sems = refs[-1]
        moves = [
            pltpu.make_async_copy(src, dst, sems.at[i])
            for i, (src, dst) in enumerate(plan(at_ref, refs[:n], refs[n:-1]))
        ]
        for move in moves:
            move.start()
        for move in moves:
            move.wait()

    return call(
        kernel, at, arrays, [pl.BlockSpec(memory_space=pltpu.HBM)] * n, outs,
        [pl.BlockSpec(out.shape, lambda i, at: (0, 0)) for out in outs],
        scratch=[pltpu.SemaphoreType.DMA((count,))], after=after, vmem=vmem,
    )


def add(at, arrays, after=()):
    rows, width = arrays[0].shape
    spec = pl.BlockSpec((rows, width // 2), lambda i, at: (0, i))

    def kernel(at_ref, *refs):
        total = refs[0][...].astype(F32)
        for ref in refs[1:-1]:
            total = total + ref[...].astype(F32)
        refs[-1][...] = total.astype(BF16)

    return call(kernel, at, arrays, [spec] * len(arrays), [shape((rows, width))], [spec], (2,), after=after)[0]


def copy_of(at, x, rows=None, after=()):
    rows = rows or x.shape[0]
    spec = pl.BlockSpec((rows // 2, x.shape[1]), lambda i, at: (i, 0))

    def kernel(at_ref, x_ref, out_ref):
        out_ref[...] = x_ref[...]

    return call(kernel, at, [x], [spec], [shape((rows, x.shape[1]))], [spec], (2,), after=after)[0]


def dot(a, b, over_a, over_b):
    return lax.dot_general(a, b, (((over_a,), (over_b,)), ((), ())), preferred_element_type=F32)


def part_rows(x, at, rows):
    return lax.dynamic_slice_in_dim(x, at * rows, rows, 0)


def piece(x, at, axis):
    return lax.dynamic_index_in_dim(x, at, axis, keepdims=False)


def body(hidden, grad_out, weight):
    row, rep = lax.axis_index("row"), lax.axis_index("rep")
    y, x_hi = row // 2, row % 2
    x_lo, core = rep // 2, rep % 2
    first = y ^ (1 + 2 * core)
    second = y ^ (3 - 2 * core)
    z = lax.axis_index("col")
    cols = lax.axis_size("col")
    bits = [1 << i for i in reversed(range(cols.bit_length() - 1))]
    at = jnp.stack([y, second, first, y ^ 2, rep, rep ^ 1, rep ^ 2, rep ^ 3, core, x_lo, x_hi, *[z // bit % 2 for bit in bits]]).astype(jnp.int32)
    tokens, tile_rows = hidden.shape
    slab = weight.shape[1]
    half = tile_rows // 2
    pair = 2 * slab
    n = GATHERED_ROWS
    rest = half - n
    chunk = tile_rows // A_CHUNKS
    quarter = tokens // N_Y
    half_tiles, n_tiles, chunk_tiles = half // TILE, n // TILE, chunk // TILE

    hidden_c, grad_out_c, weight_c = (send(x, CORE) for x in (hidden, grad_out, weight))
    weight_x = [send(weight[:chunk], X_LO)]
    first_cut, low = (n_tiles - 1) * TILE, (n_tiles + 1) // 2 * TILE
    cuts = [(0, 0, first_cut), (0, first_cut, n - first_cut), (1, 0, low), (1, low, n - low)]

    def hidden_moves(at, hidden_ref, out, cut):
        other, start, size = cut
        start = pl.multiple_of((1 - at[CORE_AT] if other else at[CORE_AT]) * half, TILE) + start
        step = tokens // 4
        return [
            (hidden_ref.at[pl.ds(j * step, step), pl.ds(start, size)], out.at[pl.ds(j * step, step)])
            for j in range(4)
        ]

    cut_shapes = [shape((tokens, size)) for _, _, size in cuts]
    hidden_sent = copies(
        at, [hidden], cut_shapes[:1], lambda at, ins, outs: hidden_moves(at, ins[0], outs[0], cuts[0]), 4
    )
    hidden_x = [send(hidden_sent[0], X_OUT)]
    *hidden_late, weight_late = copies(
        at, [hidden, weight], cut_shapes[1:] + [shape((chunk, slab))],
        lambda at, ins, outs: [
            *hidden_moves(at, ins[0], outs[0], cuts[1]), *hidden_moves(at, ins[0], outs[1], cuts[2]),
            *hidden_moves(at, ins[0], outs[2], cuts[3]), (ins[1].at[pl.ds(chunk, chunk)], outs[3]),
        ], 13, after=hidden_sent,
    )
    weight_x.append(send(weight_late, X_LO))
    hidden_x += [send(h, p) for h, p in zip(hidden_late, (X_OUT, X_OUT_CORE, X_OUT_CORE))]

    def turn_plan(at, ins, outs):
        moves = []
        for i, p in enumerate((Y, SECOND, FIRST, FAR)):
            for j, s in enumerate((SLAB, SLAB_C, SLAB_X, SLAB_XC)):
                src = ins[0].at[
                    pl.ds(pl.multiple_of(at[p] * quarter, quarter), quarter),
                    pl.ds(pl.multiple_of(at[s] * slab, slab), slab),
                ]
                moves.append((src, outs[0].at[pl.ds(i * quarter, quarter), pl.ds(j * slab, slab)]))
        return moves

    turned = copies(at, [grad_out], [shape(grad_out.shape)], turn_plan, 16, after=[weight_late])[0]

    def sum_kernel(at, hidden_ref, hidden_c_ref, out_ref, out_c_ref, result_ref):
        result_ref[...] = dot(hidden_ref[...], out_ref[...], 0, 0) + dot(hidden_c_ref[...], out_c_ref[...], 0, 0)

    tile_spec = pl.BlockSpec((TILE, pair), lambda i, at: (i, 0))
    own_columns = pl.BlockSpec((tokens, pair), lambda i, at: (0, at[X_LO_AT]))
    own_sum = call(
        sum_kernel, at, [hidden, hidden_c, grad_out, grad_out_c],
        [
            pl.BlockSpec((tokens, TILE), lambda i, at: (0, at[CORE_AT] * half_tiles + i)),
            pl.BlockSpec((tokens, TILE), lambda i, at: (0, at[CORE_AT] * half_tiles + i)),
            own_columns, own_columns,
        ],
        [shape((half, pair), F32)], [tile_spec], (half_tiles,), after=[turned],
    )[0]

    lead = tokens // TILE

    def away_kernel(at, hidden_ref, hidden_c_ref, out_ref, out_c_ref, result_ref):
        i = pl.program_id(0)

        @pl.when(i < lead)
        def _():
            result_ref[...] = out_ref[pl.ds(pl.multiple_of(i * TILE, TILE), TILE)]

        @pl.when(i >= lead)
        def _():
            total = dot(hidden_ref[...], out_ref[...], 0, 0) + dot(hidden_c_ref[...], out_c_ref[...], 0, 0)
            result_ref[...] = total.astype(BF16)

    def send_away(after):
        columns = pl.BlockSpec((tokens, pair), lambda i, at: (0, 1 - at[X_LO_AT]))
        tile = lambda i: n_tiles + jnp.maximum(i - lead, 0)
        away = call(
            away_kernel, at, [hidden, hidden_c, grad_out, grad_out_c],
            [
                pl.BlockSpec((tokens, TILE), lambda i, at: (0, at[CORE_AT] * half_tiles + tile(i))),
                pl.BlockSpec((tokens, TILE), lambda i, at: (0, at[CORE_AT] * half_tiles + tile(i))),
                columns, columns,
            ],
            [shape((tokens + rest, pair))], [tile_spec], (lead + rest // TILE,), after=after,
        )[0]
        return away, send(away, X_LO)

    def width_kernel(at, turned_ref, *refs):
        total = 0.0
        for j in range(4):
            total = total + dot(turned_ref[:, j * slab:(j + 1) * slab], refs[j][...], 1, 1)
        for i in range(N_Y):
            refs[4 + i][...] = total[i * quarter:(i + 1) * quarter].astype(BF16)

    def scatter_sends(own, near, off, opposite):
        return own, near, send(opposite, Y_FIRST), send(off, Y_FIRST)

    def width_parts(k, after):
        forward = copy_of(at, weight_x[k], after=after)
        step = chunk // 2
        here = pl.BlockSpec((step, slab), lambda i, at: (2 * k + i, 0))
        there = pl.BlockSpec((step, slab), lambda i, at: (i, 0))
        return forward, lambda after: call(
            width_kernel, at, [turned, weight, weight_c, weight_x[k], send(forward, CORE)],
            [pl.BlockSpec(turned.shape, lambda i, at: (0, 0)), here, here, there, there],
            [shape((quarter, chunk))] * N_Y,
            [pl.BlockSpec((quarter, step), lambda i, at: (0, i))] * N_Y,
            (2,), after=after, vmem=16,
        )

    away, came_away = send_away([own_sum])
    forward, parts = width_parts(0, [away, hidden_x[0]])
    own, near, came_near, came_own = scatter_sends(*parts([forward]))
    near = add(at, [near, came_near])
    mine = [add(at, [own, came_own, send(near, Y_SECOND)])]
    forward, parts = width_parts(1, [mine[0], hidden_x[2]])
    own, near, came_near, came_own = scatter_sends(*parts([forward]))
    near = add(at, [near, came_near])
    mine.append(add(at, [own, came_own, send(near, Y_SECOND)]))
    beside = [send(m, X_HI) for m in mine]
    out_came = copy_of(at, came_away, tokens, after=[mine[1], hidden_x[1], hidden_x[3]])
    out_xc = send(out_came, CORE)

    def grad_kernel(at, sum_ref, a_low, a_high, b_low, b_high, out_x_ref, out_xc_ref, came_ref, result_ref):
        i = pl.program_id(0)

        def gathered(a_ref, b_ref):
            total = sum_ref[...] + dot(a_ref[...], out_x_ref[...], 0, 0)
            result_ref[...] = (total + dot(b_ref[...], out_xc_ref[...], 0, 0)).astype(BF16)

        bounds = [0, low // TILE, first_cut // TILE, n_tiles]
        for j, refs in enumerate(((a_low, b_low), (a_low, b_high), (a_high, b_high))):

            @pl.when((i >= bounds[j]) & (i < bounds[j + 1]))
            def _():
                gathered(*refs)

        @pl.when(i >= n_tiles)
        def _():
            result_ref[...] = (sum_ref[...] + came_ref[...].astype(F32)).astype(BF16)

    def cut_spec(start, size):
        return pl.BlockSpec(
            (tokens, TILE), lambda i, at: (0, jnp.clip(i - start // TILE, 0, size // TILE - 1))
        )

    all_out = pl.BlockSpec((tokens, pair), lambda i, at: (0, 0))
    own_half = call(
        grad_kernel, at, [own_sum, *hidden_x, came_away, out_xc, came_away],
        [
            tile_spec, *[cut_spec(start, size) for _, start, size in cuts], all_out, all_out,
            pl.BlockSpec((TILE, pair), lambda i, at: (lead + jnp.maximum(i - n_tiles, 0), 0)),
        ],
        [shape((half, pair))], [tile_spec], (half_tiles,), after=mine,
    )[0]
    other_half = send(own_half, CORE)

    num = tile_rows // BLK
    mine_rows = BLK // 2 // N_Y

    def left_kernel(at, own_low, own_high, other_low, other_high, *refs):
        outs, block, product = refs[:N_Y], refs[N_Y], refs[N_Y + 1]
        a = pl.program_id(0)
        for part, own_ref, other_ref in ((0, own_low, other_low), (1, own_high, other_high)):
            held = (2 * a + part) // half_tiles == at[CORE_AT]
            block[part * TILE:(part + 1) * TILE] = jnp.where(held, own_ref[...], other_ref[...])
        groups = block[...].reshape(16, 2, 16, pair)
        my_rows = jnp.where(at[CORE_AT] == 0, groups[:, 0], groups[:, 1]).reshape(BLK // 2, pair)
        product[...] = (dot(my_rows, block[...], 1, 1) / D).astype(BF16)
        for i, p in enumerate((Y, SECOND, FIRST, FAR)):
            outs[i][0] = product[pl.ds(pl.multiple_of(at[p] * mine_rows, mine_rows), mine_rows)]

    halves = [
        pl.BlockSpec((TILE, pair), lambda a, at, part=part: ((2 * a + part) % half_tiles, 0)) for part in (0, 1)
    ]
    left = left_parts = call(
        left_kernel, at, [own_half, own_half, other_half, other_half], halves + halves,
        [shape((num, mine_rows, BLK))] * N_Y,
        [pl.BlockSpec((1, mine_rows, BLK), lambda a, at: (a, 0, 0))] * N_Y,
        (num,), scratch=[pltpu.VMEM((BLK, pair), BF16), pltpu.VMEM((BLK // 2, BLK), BF16)],
        after=[own_half],
    )
    totals = [add(at, [mine[0], beside[0]], after=left_parts[:1])]
    def slab_kernel(at, own_ref, other_ref, result_ref, token_ref):
        token_ref[...] = jnp.zeros_like(token_ref)
        held = pl.program_id(0) == at[CORE_AT]
        result_ref[...] = jnp.where(held, own_ref[...], other_ref[...])

    slab_half = pl.BlockSpec((half, slab), lambda i, at: (0, at[CORE_AT]))
    grad_slab, slab_done = call(
        slab_kernel, at, [own_half, other_half], [slab_half] * 2, [shape(weight.shape), shape((8, 128), F32)],
        [pl.BlockSpec((half, slab), lambda i, at: (i, 0)), pl.BlockSpec((8, 128), lambda i, at: (0, 0))],
        (2,), after=totals,
    )

    own, near, came_near, came_own = scatter_sends(*left)

    def place_kernel(at, *refs):
        refs[-1][...] = jnp.zeros_like(refs[-1])
        for j in range(N_Y):

            @pl.when(pl.program_id(0) == j)
            def _():
                refs[-2][...] = refs[j][...]

    def go_round(k, total, grad_hidden, after):
        near = send(total, Y_SECOND)
        off = send(total, Y_FIRST)
        opposite = send(near, Y_FIRST)
        given = [total, near, off, opposite]
        specs = [pl.BlockSpec(total.shape, lambda i, at: (0, 0))] * N_Y
        if k > 0:
            given, specs = given + [grad_hidden], specs + [ANY]
        return call(
            place_kernel, at, given, specs, [shape(hidden.shape), shape((8, 128), F32)],
            [
                pl.BlockSpec(total.shape, lambda i, at: (at[Y + i], k)),
                pl.BlockSpec((8, 128), lambda i, at: (0, 0)),
            ],
            (N_Y,), aliases={N_Y + 1: 0} if k > 0 else None, after=after,
        )

    blocks = (num * mine_rows, BLK)
    near = add(at, [near.reshape(blocks), came_near.reshape(blocks)], after=[slab_done, came_own, beside[1]])
    totals.append(add(at, [mine[1], beside[1]], after=[near]))
    grad_hidden, placed = go_round(0, totals[0], None, [totals[1]])
    upper = pair // 2

    def right_kernel(at, own_ref, other_ref, own_slab_ref, other_slab_ref, keep_ref, send_ref, total_ref):
        i = pl.program_id(0)
        value = dot(own_ref[...], own_slab_ref[...], 0, 0) + dot(other_ref[...], other_slab_ref[...], 0, 0)

        @pl.when(i == 0)
        def _():
            total_ref[...] = value

        @pl.when(i > 0)
        def _():
            total_ref[...] += value

        @pl.when(i == pl.num_programs(0) - 1)
        def _():
            here = at[Z_HIGH] * upper
            there = (1 - at[Z_HIGH]) * upper
            keep_ref[...] = total_ref[pl.ds(pl.multiple_of(here, upper), upper)] / FF
            send_ref[...] = (total_ref[pl.ds(pl.multiple_of(there, upper), upper)] / FF).astype(BF16)

    steps = 2
    rows_spec = pl.BlockSpec((half // steps, pair), lambda i, at: (i, 0))
    slab_spec = pl.BlockSpec((half // steps, slab), lambda i, at: (i, at[CORE_AT]))
    upper_spec = pl.BlockSpec((upper, slab), lambda i, at: (0, 0))

    stay, go = call(
        right_kernel, at, [own_half, other_half, own_half, other_half],
        [rows_spec, rows_spec, slab_spec, slab_spec],
        [shape((upper, slab), F32), shape((upper, slab))], [upper_spec] * 2, (steps,),
        scratch=[pltpu.VMEM((pair, slab), F32)], after=totals[1:],
    )

    def right_sum(stay, came, bit):
        rows = stay.shape[0] // 2

        def kernel(at_ref, stay_ref, came_ref, keep_ref, send_ref):
            total = stay_ref[...] + came_ref[...].astype(F32)
            here = at_ref[bit] == 0
            keep_ref[...] = jnp.where(here, total[:rows], total[rows:])
            send_ref[...] = jnp.where(here, total[rows:], total[:rows]).astype(BF16)

        whole = pl.BlockSpec(stay.shape, lambda i, at: (0, 0))
        half_of = pl.BlockSpec((rows, slab), lambda i, at: (0, 0))
        return call(
            kernel, at, [stay, came], [whole] * 2, [shape((rows, slab), F32), shape((rows, slab))], [half_of] * 2
        )

    right_steps = []
    for i, bit in enumerate(bits):
        came_z = lax.ppermute(go, "col", [(j, j ^ bit) for j in range(cols)])
        if i < len(bits) - 1:
            stay, go = right_sum(stay, came_z, Z_HIGH + 1 + i)
            right_steps.append(stay)

    near = near.reshape(own.shape)
    def left_sum(parts, groups, bit, after=()):
        def kernel(at_ref, *refs):
            total = refs[0][...].astype(F32)
            for ref in refs[1:-2]:
                total = total + ref[...].astype(F32)
            total = total.reshape((num * groups // 2, 2, 16, BLK))
            stays = at_ref[bit] == 0
            rows = (num, groups * 8, BLK)
            refs[-2][...] = jnp.where(stays, total[:, 0], total[:, 1]).reshape(rows)
            refs[-1][...] = jnp.where(stays, total[:, 1], total[:, 0]).reshape(rows).astype(BF16)

        whole = pl.BlockSpec((num, groups * 16, BLK), lambda a, at: (0, 0, 0))
        half_of = pl.BlockSpec((num, groups * 8, BLK), lambda a, at: (0, 0, 0))
        return call(
            kernel, at, parts, [whole] * len(parts),
            [shape((num, groups * 8, BLK), F32), shape((num, groups * 8, BLK))], [half_of] * 2, after=after,
        )

    stays, goes = left_sum([own, came_own, send(near, Y_SECOND)], 4, X_LO_AT)
    stays, goes = left_sum([stays, send(goes, X_LO)], 2, X_HI_AT)
    left_stats = stays + send(goes, X_HI).astype(F32)

    def last_kernel(at, mine_ref, came_ref, result_ref):
        result_ref[...] = mine_ref[...] + came_ref[...].astype(F32)

    spec = pl.BlockSpec(stay.shape, lambda i, at: (0, 0))
    right_stats = call(
        last_kernel, at, [stay, came_z], [spec] * 2, [shape(stay.shape, F32)], [spec], after=[placed]
    )[0].T

    grad_hidden, _ = go_round(1, totals[1], grad_hidden, [left_stats, right_stats])
    return grad_hidden, grad_slab, left_stats, right_stats


def solution(mesh):
    return jax.shard_map(
        body,
        mesh=mesh,
        in_specs=(P("rep", "col"), P("rep", "row"), P("col", ("row", "rep"))),
        out_specs=(
            P("rep", "col"),
            P("col", ("row", "rep")),
            P("col", ("row", "rep"), None),
            P(("row", "rep"), "col"),
        ),
        check_vma=False,
    )
```

```python
import jax
import jax.numpy as jnp
from jax import lax
from jax.experimental import pallas as pl
from jax.experimental.pallas import tpu as pltpu
from jax.sharding import PartitionSpec as P

D = 8192
FF = 28672
BLK = 512
N_Y = 4
A_CHUNKS = 2
GATHERED_ROWS = 1280
TILE = 256
F32 = jnp.float32
BF16 = jnp.bfloat16

Y, SECOND, FIRST, FAR, SLAB, SLAB_C, SLAB_X, SLAB_XC, CORE_AT, X_LO_AT, X_HI_AT, Z_HIGH = range(12)


def plane_perm(move):
    pairs = []
    for at in range(32):
        y, x_hi, x_lo, core = at // 8, at // 4 % 2, at // 2 % 2, at % 2
        y, x_hi, x_lo, core = move(y, x_hi, x_lo, core)
        pairs.append((at, y * 8 + x_hi * 4 + x_lo * 2 + core))
    return pairs


CORE = plane_perm(lambda y, h, l, c: (y, h, l, 1 - c))
X_LO = plane_perm(lambda y, h, l, c: (y, h, 1 - l, c))
X_HI = plane_perm(lambda y, h, l, c: (y, 1 - h, l, c))
X_OUT = plane_perm(lambda y, h, l, c: (y, 1 - h, 1 - l, c))
X_OUT_CORE = plane_perm(lambda y, h, l, c: (y, 1 - h, 1 - l, 1 - c))
Y_FIRST = plane_perm(lambda y, h, l, c: (y ^ (3 if c else 1), h, l, c))
Y_SECOND = plane_perm(lambda y, h, l, c: (y ^ (1 if c else 3), h, l, c))


def send(x, perm):
    return lax.ppermute(x, ("row", "rep"), perm)


def shape(dims, dtype=BF16):
    return jax.ShapeDtypeStruct(dims, dtype)


ANY = pl.BlockSpec(memory_space=pl.ANY)


def call(kernel, at, arrays, in_specs, outs, out_specs, grid=(1,), scratch=(), after=(), aliases=None, vmem=10):
    n, m = len(arrays), len(after)

    def run(at_ref, *refs):
        kernel(at_ref, *refs[:n], *refs[n + m:])

    return pl.pallas_call(
        run,
        grid_spec=pltpu.PrefetchScalarGridSpec(
            num_scalar_prefetch=1,
            grid=grid,
            in_specs=list(in_specs) + [ANY] * m,
            out_specs=list(out_specs),
            scratch_shapes=list(scratch),
        ),
        out_shape=list(outs),
        input_output_aliases=aliases or {},
        compiler_params=pltpu.CompilerParams(vmem_limit_bytes=vmem * 2**20),
        cost_estimate=pl.CostEstimate(flops=1, bytes_accessed=1, transcendentals=0),
    )(at, *arrays, *after)


def copies(at, arrays, outs, plan, count, after=(), vmem=16):
    n = len(arrays)

    def kernel(at_ref, *refs):
        sems = refs[-1]
        moves = [
            pltpu.make_async_copy(src, dst, sems.at[i])
            for i, (src, dst) in enumerate(plan(at_ref, refs[:n], refs[n:-1]))
        ]
        for move in moves:
            move.start()
        for move in moves:
            move.wait()

    return call(
        kernel, at, arrays, [pl.BlockSpec(memory_space=pltpu.HBM)] * n, outs,
        [pl.BlockSpec(out.shape, lambda i, at: (0, 0)) for out in outs],
        scratch=[pltpu.SemaphoreType.DMA((count,))], after=after, vmem=vmem,
    )


def add(at, arrays, after=()):
    rows, width = arrays[0].shape
    spec = pl.BlockSpec((rows, width // 2), lambda i, at: (0, i))

    def kernel(at_ref, *refs):
        total = refs[0][...].astype(F32)
        for ref in refs[1:-1]:
            total = total + ref[...].astype(F32)
        refs[-1][...] = total.astype(BF16)

    return call(kernel, at, arrays, [spec] * len(arrays), [shape((rows, width))], [spec], (2,), after=after)[0]


def copy_of(at, x, rows=None, after=()):
    rows = rows or x.shape[0]
    spec = pl.BlockSpec((rows // 2, x.shape[1]), lambda i, at: (i, 0))

    def kernel(at_ref, x_ref, out_ref):
        out_ref[...] = x_ref[...]

    return call(kernel, at, [x], [spec], [shape((rows, x.shape[1]))], [spec], (2,), after=after)[0]


def dot(a, b, over_a, over_b):
    return lax.dot_general(a, b, (((over_a,), (over_b,)), ((), ())), preferred_element_type=F32)


def part_rows(x, at, rows):
    return lax.dynamic_slice_in_dim(x, at * rows, rows, 0)


def piece(x, at, axis):
    return lax.dynamic_index_in_dim(x, at, axis, keepdims=False)


def body(hidden, grad_out, weight):
    row, rep = lax.axis_index("row"), lax.axis_index("rep")
    y, x_hi = row // 2, row % 2
    x_lo, core = rep // 2, rep % 2
    first = y ^ (1 + 2 * core)
    second = y ^ (3 - 2 * core)
    z = lax.axis_index("col")
    cols = lax.axis_size("col")
    bits = [1 << i for i in reversed(range(cols.bit_length() - 1))]
    at = jnp.stack([y, second, first, y ^ 2, rep, rep ^ 1, rep ^ 2, rep ^ 3, core, x_lo, x_hi, *[z // bit % 2 for bit in bits]]).astype(jnp.int32)
    tokens, tile_rows = hidden.shape
    slab = weight.shape[1]
    half = tile_rows // 2
    pair = 2 * slab
    n = GATHERED_ROWS
    rest = half - n
    chunk = tile_rows // A_CHUNKS
    quarter = tokens // N_Y
    half_tiles, n_tiles, chunk_tiles = half // TILE, n // TILE, chunk // TILE

    hidden_c, grad_out_c, weight_c = (send(x, CORE) for x in (hidden, grad_out, weight))
    weight_x = [send(weight[:chunk], X_LO)]
    first_cut, low = (n_tiles - 1) * TILE, (n_tiles + 1) // 2 * TILE
    cuts = [(0, 0, first_cut), (0, first_cut, n - first_cut), (1, 0, low), (1, low, n - low)]

    def hidden_moves(at, hidden_ref, out, cut):
        other, start, size = cut
        start = pl.multiple_of((1 - at[CORE_AT] if other else at[CORE_AT]) * half, TILE) + start
        step = tokens // 4
        return [
            (hidden_ref.at[pl.ds(j * step, step), pl.ds(start, size)], out.at[pl.ds(j * step, step)])
            for j in range(4)
        ]

    cut_shapes = [shape((tokens, size)) for _, _, size in cuts]
    hidden_sent = copies(
        at, [hidden], cut_shapes[:1], lambda at, ins, outs: hidden_moves(at, ins[0], outs[0], cuts[0]), 4
    )
    hidden_x = [send(hidden_sent[0], X_OUT)]
    *hidden_late, weight_late = copies(
        at, [hidden, weight], cut_shapes[1:] + [shape((chunk, slab))],
        lambda at, ins, outs: [
            *hidden_moves(at, ins[0], outs[0], cuts[1]), *hidden_moves(at, ins[0], outs[1], cuts[2]),
            *hidden_moves(at, ins[0], outs[2], cuts[3]), (ins[1].at[pl.ds(chunk, chunk)], outs[3]),
        ], 13, after=hidden_sent,
    )
    weight_x.append(send(weight_late, X_LO))
    hidden_x += [send(h, p) for h, p in zip(hidden_late, (X_OUT, X_OUT_CORE, X_OUT_CORE))]

    def turn_plan(at, ins, outs):
        moves = []
        for i, p in enumerate((Y, SECOND, FIRST, FAR)):
            for j, s in enumerate((SLAB, SLAB_C, SLAB_X, SLAB_XC)):
                src = ins[0].at[
                    pl.ds(pl.multiple_of(at[p] * quarter, quarter), quarter),
                    pl.ds(pl.multiple_of(at[s] * slab, slab), slab),
                ]
                moves.append((src, outs[0].at[pl.ds(i * quarter, quarter), pl.ds(j * slab, slab)]))
        return moves

    turned = copies(at, [grad_out], [shape(grad_out.shape)], turn_plan, 16, after=[weight_late])[0]

    def sum_kernel(at, hidden_ref, hidden_c_ref, out_ref, out_c_ref, result_ref):
        result_ref[...] = dot(hidden_ref[...], out_ref[...], 0, 0) + dot(hidden_c_ref[...], out_c_ref[...], 0, 0)

    tile_spec = pl.BlockSpec((TILE, pair), lambda i, at: (i, 0))
    own_columns = pl.BlockSpec((tokens, pair), lambda i, at: (0, at[X_LO_AT]))
    own_sum = call(
        sum_kernel, at, [hidden, hidden_c, grad_out, grad_out_c],
        [
            pl.BlockSpec((tokens, TILE), lambda i, at: (0, at[CORE_AT] * half_tiles + i)),
            pl.BlockSpec((tokens, TILE), lambda i, at: (0, at[CORE_AT] * half_tiles + i)),
            own_columns, own_columns,
        ],
        [shape((half, pair), F32)], [tile_spec], (half_tiles,), after=[turned],
    )[0]

    lead = tokens // TILE

    def away_kernel(at, hidden_ref, hidden_c_ref, out_ref, out_c_ref, result_ref):
        i = pl.program_id(0)

        @pl.when(i < lead)
        def _():
            result_ref[...] = out_ref[pl.ds(pl.multiple_of(i * TILE, TILE), TILE)]

        @pl.when(i >= lead)
        def _():
            total = dot(hidden_ref[...], out_ref[...], 0, 0) + dot(hidden_c_ref[...], out_c_ref[...], 0, 0)
            result_ref[...] = total.astype(BF16)

    def send_away(after):
        columns = pl.BlockSpec((tokens, pair), lambda i, at: (0, 1 - at[X_LO_AT]))
        tile = lambda i: n_tiles + jnp.maximum(i - lead, 0)
        away = call(
            away_kernel, at, [hidden, hidden_c, grad_out, grad_out_c],
            [
                pl.BlockSpec((tokens, TILE), lambda i, at: (0, at[CORE_AT] * half_tiles + tile(i))),
                pl.BlockSpec((tokens, TILE), lambda i, at: (0, at[CORE_AT] * half_tiles + tile(i))),
                columns, columns,
            ],
            [shape((tokens + rest, pair))], [tile_spec], (lead + rest // TILE,), after=after,
        )[0]
        return away, send(away, X_LO)

    def width_kernel(at, turned_ref, *refs):
        total = 0.0
        for j in range(4):
            total = total + dot(turned_ref[:, j * slab:(j + 1) * slab], refs[j][...], 1, 1)
        for i in range(N_Y):
            refs[4 + i][...] = total[i * quarter:(i + 1) * quarter].astype(BF16)

    def scatter_sends(own, near, off, opposite):
        return own, near, send(opposite, Y_FIRST), send(off, Y_FIRST)

    def width_parts(k, after):
        forward = copy_of(at, weight_x[k], after=after)
        step = chunk // 2
        here = pl.BlockSpec((step, slab), lambda i, at: (2 * k + i, 0))
        there = pl.BlockSpec((step, slab), lambda i, at: (i, 0))
        return forward, lambda after: call(
            width_kernel, at, [turned, weight, weight_c, weight_x[k], send(forward, CORE)],
            [pl.BlockSpec(turned.shape, lambda i, at: (0, 0)), here, here, there, there],
            [shape((quarter, chunk))] * N_Y,
            [pl.BlockSpec((quarter, step), lambda i, at: (0, i))] * N_Y,
            (2,), after=after, vmem=16,
        )

    away, came_away = send_away([own_sum])
    forward, parts = width_parts(0, [away, hidden_x[0]])
    own, near, came_near, came_own = scatter_sends(*parts([forward]))
    near = add(at, [near, came_near])
    mine = [add(at, [own, came_own, send(near, Y_SECOND)])]
    forward, parts = width_parts(1, [mine[0], hidden_x[2]])
    own, near, came_near, came_own = scatter_sends(*parts([forward]))
    near = add(at, [near, came_near])
    mine.append(add(at, [own, came_own, send(near, Y_SECOND)]))
    beside = [send(m, X_HI) for m in mine]
    out_came = copy_of(at, came_away, tokens, after=[mine[1], hidden_x[1], hidden_x[3]])
    out_xc = send(out_came, CORE)

    def grad_kernel(at, sum_ref, a_low, a_high, b_low, b_high, out_x_ref, out_xc_ref, came_ref, result_ref):
        i = pl.program_id(0)

        def gathered(a_ref, b_ref):
            total = sum_ref[...] + dot(a_ref[...], out_x_ref[...], 0, 0)
            result_ref[...] = (total + dot(b_ref[...], out_xc_ref[...], 0, 0)).astype(BF16)

        bounds = [0, low // TILE, first_cut // TILE, n_tiles]
        for j, refs in enumerate(((a_low, b_low), (a_low, b_high), (a_high, b_high))):

            @pl.when((i >= bounds[j]) & (i < bounds[j + 1]))
            def _():
                gathered(*refs)

        @pl.when(i >= n_tiles)
        def _():
            result_ref[...] = (sum_ref[...] + came_ref[...].astype(F32)).astype(BF16)

    def cut_spec(start, size):
        return pl.BlockSpec(
            (tokens, TILE), lambda i, at: (0, jnp.clip(i - start // TILE, 0, size // TILE - 1))
        )

    all_out = pl.BlockSpec((tokens, pair), lambda i, at: (0, 0))
    own_half = call(
        grad_kernel, at, [own_sum, *hidden_x, came_away, out_xc, came_away],
        [
            tile_spec, *[cut_spec(start, size) for _, start, size in cuts], all_out, all_out,
            pl.BlockSpec((TILE, pair), lambda i, at: (lead + jnp.maximum(i - n_tiles, 0), 0)),
        ],
        [shape((half, pair))], [tile_spec], (half_tiles,), after=mine,
    )[0]
    other_half = send(own_half, CORE)

    num = tile_rows // BLK
    mine_rows = BLK // 2 // N_Y

    def left_kernel(at, own_low, own_high, other_low, other_high, *refs):
        outs, block, product = refs[:N_Y], refs[N_Y], refs[N_Y + 1]
        a = pl.program_id(0)
        for part, own_ref, other_ref in ((0, own_low, other_low), (1, own_high, other_high)):
            held = (2 * a + part) // half_tiles == at[CORE_AT]
            block[part * TILE:(part + 1) * TILE] = jnp.where(held, own_ref[...], other_ref[...])
        groups = block[...].reshape(16, 2, 16, pair)
        my_rows = jnp.where(at[CORE_AT] == 0, groups[:, 0], groups[:, 1]).reshape(BLK // 2, pair)
        product[...] = (dot(my_rows, block[...], 1, 1) / D).astype(BF16)
        for i, p in enumerate((Y, SECOND, FIRST, FAR)):
            outs[i][0] = product[pl.ds(pl.multiple_of(at[p] * mine_rows, mine_rows), mine_rows)]

    halves = [
        pl.BlockSpec((TILE, pair), lambda a, at, part=part: ((2 * a + part) % half_tiles, 0)) for part in (0, 1)
    ]
    left = left_parts = call(
        left_kernel, at, [own_half, own_half, other_half, other_half], halves + halves,
        [shape((num, mine_rows, BLK))] * N_Y,
        [pl.BlockSpec((1, mine_rows, BLK), lambda a, at: (a, 0, 0))] * N_Y,
        (num,), scratch=[pltpu.VMEM((BLK, pair), BF16), pltpu.VMEM((BLK // 2, BLK), BF16)],
        after=[own_half],
    )
    own, near, came_near, came_own = scatter_sends(*left)
    def go_round(total):
        near = send(total, Y_SECOND)
        off = send(total, Y_FIRST)
        return [total, near, off, send(near, Y_FIRST)]

    totals = [add(at, [mine[0], beside[0]], after=[came_near])]
    rounds = [go_round(totals[0])]
    def slab_kernel(at, own_ref, other_ref, result_ref, token_ref):
        token_ref[...] = jnp.zeros_like(token_ref)
        held = pl.program_id(0) == at[CORE_AT]
        result_ref[...] = jnp.where(held, own_ref[...], other_ref[...])

    slab_half = pl.BlockSpec((half, slab), lambda i, at: (0, at[CORE_AT]))
    grad_slab, slab_done = call(
        slab_kernel, at, [own_half, other_half], [slab_half] * 2, [shape(weight.shape), shape((8, 128), F32)],
        [pl.BlockSpec((half, slab), lambda i, at: (i, 0)), pl.BlockSpec((8, 128), lambda i, at: (0, 0))],
        (2,), after=totals,
    )


    def place_kernel(at, *refs):
        refs[-1][...] = jnp.zeros_like(refs[-1])
        for j in range(N_Y):

            @pl.when(pl.program_id(0) == j)
            def _():
                refs[-2][...] = refs[j][...]

    def place(k, given, grad_hidden, after):
        total = given[0]
        specs = [pl.BlockSpec(total.shape, lambda i, at: (0, 0))] * N_Y
        if k > 0:
            given, specs = given + [grad_hidden], specs + [ANY]
        return call(
            place_kernel, at, given, specs, [shape(hidden.shape), shape((8, 128), F32)],
            [
                pl.BlockSpec(total.shape, lambda i, at: (at[Y + i], k)),
                pl.BlockSpec((8, 128), lambda i, at: (0, 0)),
            ],
            (N_Y,), aliases={N_Y + 1: 0} if k > 0 else None, after=after,
        )

    blocks = (num * mine_rows, BLK)
    near = add(at, [near.reshape(blocks), came_near.reshape(blocks)], after=[slab_done, came_own, beside[1]])
    totals.append(add(at, [mine[1], beside[1]], after=[near, rounds[0][2]]))
    rounds.append(go_round(totals[1]))
    grad_hidden, placed = place(0, rounds[0], None, [totals[1]])
    upper = pair // 2

    def right_kernel(at, own_ref, other_ref, own_slab_ref, other_slab_ref, keep_ref, send_ref, total_ref):
        i = pl.program_id(0)
        value = dot(own_ref[...], own_slab_ref[...], 0, 0) + dot(other_ref[...], other_slab_ref[...], 0, 0)

        @pl.when(i == 0)
        def _():
            total_ref[...] = value

        @pl.when(i > 0)
        def _():
            total_ref[...] += value

        @pl.when(i == pl.num_programs(0) - 1)
        def _():
            here = at[Z_HIGH] * upper
            there = (1 - at[Z_HIGH]) * upper
            keep_ref[...] = total_ref[pl.ds(pl.multiple_of(here, upper), upper)] / FF
            send_ref[...] = (total_ref[pl.ds(pl.multiple_of(there, upper), upper)] / FF).astype(BF16)

    steps = 2
    rows_spec = pl.BlockSpec((half // steps, pair), lambda i, at: (i, 0))
    slab_spec = pl.BlockSpec((half // steps, slab), lambda i, at: (i, at[CORE_AT]))
    upper_spec = pl.BlockSpec((upper, slab), lambda i, at: (0, 0))

    stay, go = call(
        right_kernel, at, [own_half, other_half, own_half, other_half],
        [rows_spec, rows_spec, slab_spec, slab_spec],
        [shape((upper, slab), F32), shape((upper, slab))], [upper_spec] * 2, (steps,),
        scratch=[pltpu.VMEM((pair, slab), F32)], after=totals[1:],
    )

    def right_sum(stay, came, bit):
        rows = stay.shape[0] // 2

        def kernel(at_ref, stay_ref, came_ref, keep_ref, send_ref):
            total = stay_ref[...] + came_ref[...].astype(F32)
            here = at_ref[bit] == 0
            keep_ref[...] = jnp.where(here, total[:rows], total[rows:])
            send_ref[...] = jnp.where(here, total[rows:], total[:rows]).astype(BF16)

        whole = pl.BlockSpec(stay.shape, lambda i, at: (0, 0))
        half_of = pl.BlockSpec((rows, slab), lambda i, at: (0, 0))
        return call(
            kernel, at, [stay, came], [whole] * 2, [shape((rows, slab), F32), shape((rows, slab))], [half_of] * 2
        )

    right_steps = []
    for i, bit in enumerate(bits):
        came_z = lax.ppermute(go, "col", [(j, j ^ bit) for j in range(cols)])
        if i < len(bits) - 1:
            stay, go = right_sum(stay, came_z, Z_HIGH + 1 + i)
            right_steps.append(stay)

    near = near.reshape(own.shape)
    def left_sum(parts, groups, bit, after=()):
        def kernel(at_ref, *refs):
            total = refs[0][...].astype(F32)
            for ref in refs[1:-2]:
                total = total + ref[...].astype(F32)
            total = total.reshape((num * groups // 2, 2, 16, BLK))
            stays = at_ref[bit] == 0
            rows = (num, groups * 8, BLK)
            refs[-2][...] = jnp.where(stays, total[:, 0], total[:, 1]).reshape(rows)
            refs[-1][...] = jnp.where(stays, total[:, 1], total[:, 0]).reshape(rows).astype(BF16)

        whole = pl.BlockSpec((num, groups * 16, BLK), lambda a, at: (0, 0, 0))
        half_of = pl.BlockSpec((num, groups * 8, BLK), lambda a, at: (0, 0, 0))
        return call(
            kernel, at, parts, [whole] * len(parts),
            [shape((num, groups * 8, BLK), F32), shape((num, groups * 8, BLK))], [half_of] * 2, after=after,
        )

    stays, goes = left_sum([own, came_own, send(near, Y_SECOND)], 4, X_LO_AT, right_steps[:1])
    stays, goes = left_sum([stays, send(goes, X_LO)], 2, X_HI_AT, [*right_steps[1:], rounds[1][2]])
    left_stats = stays + send(goes, X_HI).astype(F32)

    def last_kernel(at, mine_ref, came_ref, result_ref):
        result_ref[...] = mine_ref[...] + came_ref[...].astype(F32)

    spec = pl.BlockSpec(stay.shape, lambda i, at: (0, 0))
    right_stats = call(
        last_kernel, at, [stay, came_z], [spec] * 2, [shape(stay.shape, F32)], [spec], after=[placed]
    )[0].T

    grad_hidden, _ = place(1, rounds[1], grad_hidden, [left_stats, right_stats])
    return grad_hidden, grad_slab, left_stats, right_stats


def solution(mesh):
    return jax.shard_map(
        body,
        mesh=mesh,
        in_specs=(P("rep", "col"), P("rep", "row"), P("col", ("row", "rep"))),
        out_specs=(
            P("rep", "col"),
            P("col", ("row", "rep")),
            P("col", ("row", "rep"), None),
            P(("row", "rep"), "col"),
        ),
        check_vma=False,
    )
```

```python
import jax
import jax.numpy as jnp
from jax import lax
from jax.experimental import pallas as pl
from jax.experimental.pallas import tpu as pltpu
from jax.sharding import PartitionSpec as P

D = 8192
FF = 28672
BLK = 512
N_Y = 4
A_CHUNKS = 2
GATHERED_ROWS = 1280
TILE = 256
F32 = jnp.float32
BF16 = jnp.bfloat16

Y, SECOND, FIRST, FAR, SLAB, SLAB_C, SLAB_X, SLAB_XC, CORE_AT, X_LO_AT, X_HI_AT, Z_HIGH = range(12)


def plane_perm(move):
    pairs = []
    for at in range(32):
        y, x_hi, x_lo, core = at // 8, at // 4 % 2, at // 2 % 2, at % 2
        y, x_hi, x_lo, core = move(y, x_hi, x_lo, core)
        pairs.append((at, y * 8 + x_hi * 4 + x_lo * 2 + core))
    return pairs


CORE = plane_perm(lambda y, h, l, c: (y, h, l, 1 - c))
X_LO = plane_perm(lambda y, h, l, c: (y, h, 1 - l, c))
X_HI = plane_perm(lambda y, h, l, c: (y, 1 - h, l, c))
X_OUT = plane_perm(lambda y, h, l, c: (y, 1 - h, 1 - l, c))
X_OUT_CORE = plane_perm(lambda y, h, l, c: (y, 1 - h, 1 - l, 1 - c))
Y_FIRST = plane_perm(lambda y, h, l, c: (y ^ (3 if c else 1), h, l, c))
Y_SECOND = plane_perm(lambda y, h, l, c: (y ^ (1 if c else 3), h, l, c))


def send(x, perm):
    return lax.ppermute(x, ("row", "rep"), perm)


def shape(dims, dtype=BF16):
    return jax.ShapeDtypeStruct(dims, dtype)


ANY = pl.BlockSpec(memory_space=pl.ANY)


def call(kernel, at, arrays, in_specs, outs, out_specs, grid=(1,), scratch=(), after=(), aliases=None, vmem=10):
    n, m = len(arrays), len(after)

    def run(at_ref, *refs):
        kernel(at_ref, *refs[:n], *refs[n + m:])

    return pl.pallas_call(
        run,
        grid_spec=pltpu.PrefetchScalarGridSpec(
            num_scalar_prefetch=1,
            grid=grid,
            in_specs=list(in_specs) + [ANY] * m,
            out_specs=list(out_specs),
            scratch_shapes=list(scratch),
        ),
        out_shape=list(outs),
        input_output_aliases=aliases or {},
        compiler_params=pltpu.CompilerParams(vmem_limit_bytes=vmem * 2**20),
        cost_estimate=pl.CostEstimate(flops=1, bytes_accessed=1, transcendentals=0),
    )(at, *arrays, *after)


def copies(at, arrays, outs, plan, count, after=(), vmem=16):
    n = len(arrays)

    def kernel(at_ref, *refs):
        sems = refs[-1]
        moves = [
            pltpu.make_async_copy(src, dst, sems.at[i])
            for i, (src, dst) in enumerate(plan(at_ref, refs[:n], refs[n:-1]))
        ]
        for move in moves:
            move.start()
        for move in moves:
            move.wait()

    return call(
        kernel, at, arrays, [pl.BlockSpec(memory_space=pltpu.HBM)] * n, outs,
        [pl.BlockSpec(out.shape, lambda i, at: (0, 0)) for out in outs],
        scratch=[pltpu.SemaphoreType.DMA((count,))], after=after, vmem=vmem,
    )


def add(at, arrays, after=()):
    rows, width = arrays[0].shape
    spec = pl.BlockSpec((rows, width // 2), lambda i, at: (0, i))

    def kernel(at_ref, *refs):
        total = refs[0][...].astype(F32)
        for ref in refs[1:-1]:
            total = total + ref[...].astype(F32)
        refs[-1][...] = total.astype(BF16)

    return call(kernel, at, arrays, [spec] * len(arrays), [shape((rows, width))], [spec], (2,), after=after)[0]


def copy_of(at, x, rows=None, after=()):
    rows = rows or x.shape[0]
    spec = pl.BlockSpec((rows // 2, x.shape[1]), lambda i, at: (i, 0))

    def kernel(at_ref, x_ref, out_ref):
        out_ref[...] = x_ref[...]

    return call(kernel, at, [x], [spec], [shape((rows, x.shape[1]))], [spec], (2,), after=after)[0]


def dot(a, b, over_a, over_b):
    return lax.dot_general(a, b, (((over_a,), (over_b,)), ((), ())), preferred_element_type=F32)


def part_rows(x, at, rows):
    return lax.dynamic_slice_in_dim(x, at * rows, rows, 0)


def piece(x, at, axis):
    return lax.dynamic_index_in_dim(x, at, axis, keepdims=False)


def body(hidden, grad_out, weight):
    row, rep = lax.axis_index("row"), lax.axis_index("rep")
    y, x_hi = row // 2, row % 2
    x_lo, core = rep // 2, rep % 2
    first = y ^ (1 + 2 * core)
    second = y ^ (3 - 2 * core)
    z = lax.axis_index("col")
    cols = lax.axis_size("col")
    bits = [1 << i for i in reversed(range(cols.bit_length() - 1))]
    at = jnp.stack([y, second, first, y ^ 2, rep, rep ^ 1, rep ^ 2, rep ^ 3, core, x_lo, x_hi, *[z // bit % 2 for bit in bits]]).astype(jnp.int32)
    tokens, tile_rows = hidden.shape
    slab = weight.shape[1]
    half = tile_rows // 2
    pair = 2 * slab
    n = GATHERED_ROWS
    rest = half - n
    chunk = tile_rows // A_CHUNKS
    quarter = tokens // N_Y
    half_tiles, n_tiles, chunk_tiles = half // TILE, n // TILE, chunk // TILE

    hidden_c, grad_out_c, weight_c = (send(x, CORE) for x in (hidden, grad_out, weight))
    weight_x = [send(weight[:chunk], X_LO)]
    first_cut, low = (n_tiles - 1) * TILE, (n_tiles + 1) // 2 * TILE
    cuts = [(0, 0, first_cut), (0, first_cut, n - first_cut), (1, 0, low), (1, low, n - low)]

    def hidden_moves(at, hidden_ref, out, cut):
        other, start, size = cut
        start = pl.multiple_of((1 - at[CORE_AT] if other else at[CORE_AT]) * half, TILE) + start
        step = tokens // 4
        return [
            (hidden_ref.at[pl.ds(j * step, step), pl.ds(start, size)], out.at[pl.ds(j * step, step)])
            for j in range(4)
        ]

    cut_shapes = [shape((tokens, size)) for _, _, size in cuts]
    hidden_sent = copies(
        at, [hidden], cut_shapes[:1], lambda at, ins, outs: hidden_moves(at, ins[0], outs[0], cuts[0]), 4
    )
    hidden_x = [send(hidden_sent[0], X_OUT)]
    *hidden_late, weight_late = copies(
        at, [hidden, weight], cut_shapes[1:] + [shape((chunk, slab))],
        lambda at, ins, outs: [
            *hidden_moves(at, ins[0], outs[0], cuts[1]), *hidden_moves(at, ins[0], outs[1], cuts[2]),
            *hidden_moves(at, ins[0], outs[2], cuts[3]), (ins[1].at[pl.ds(chunk, chunk)], outs[3]),
        ], 13, after=hidden_sent,
    )
    weight_x.append(send(weight_late, X_LO))
    hidden_x += [send(h, p) for h, p in zip(hidden_late, (X_OUT, X_OUT_CORE, X_OUT_CORE))]

    def turn_plan(at, ins, outs):
        moves = []
        for i, p in enumerate((Y, SECOND, FIRST, FAR)):
            for j, s in enumerate((SLAB, SLAB_C, SLAB_X, SLAB_XC)):
                src = ins[0].at[
                    pl.ds(pl.multiple_of(at[p] * quarter, quarter), quarter),
                    pl.ds(pl.multiple_of(at[s] * slab, slab), slab),
                ]
                moves.append((src, outs[0].at[pl.ds(i * quarter, quarter), pl.ds(j * slab, slab)]))
        return moves

    turned = copies(at, [grad_out], [shape(grad_out.shape)], turn_plan, 16, after=[weight_late])[0]

    def sum_kernel(at, hidden_ref, hidden_c_ref, out_ref, out_c_ref, result_ref):
        result_ref[...] = dot(hidden_ref[...], out_ref[...], 0, 0) + dot(hidden_c_ref[...], out_c_ref[...], 0, 0)

    tile_spec = pl.BlockSpec((TILE, pair), lambda i, at: (i, 0))
    own_columns = pl.BlockSpec((tokens, pair), lambda i, at: (0, at[X_LO_AT]))
    own_sum = call(
        sum_kernel, at, [hidden, hidden_c, grad_out, grad_out_c],
        [
            pl.BlockSpec((tokens, TILE), lambda i, at: (0, at[CORE_AT] * half_tiles + i)),
            pl.BlockSpec((tokens, TILE), lambda i, at: (0, at[CORE_AT] * half_tiles + i)),
            own_columns, own_columns,
        ],
        [shape((half, pair), F32)], [tile_spec], (half_tiles,), after=[turned],
    )[0]

    lead = tokens // TILE

    def away_kernel(at, hidden_ref, hidden_c_ref, out_ref, out_c_ref, result_ref):
        i = pl.program_id(0)

        @pl.when(i < lead)
        def _():
            result_ref[...] = out_ref[pl.ds(pl.multiple_of(i * TILE, TILE), TILE)]

        @pl.when(i >= lead)
        def _():
            total = dot(hidden_ref[...], out_ref[...], 0, 0) + dot(hidden_c_ref[...], out_c_ref[...], 0, 0)
            result_ref[...] = total.astype(BF16)

    def send_away(after):
        columns = pl.BlockSpec((tokens, pair), lambda i, at: (0, 1 - at[X_LO_AT]))
        tile = lambda i: n_tiles + jnp.maximum(i - lead, 0)
        away = call(
            away_kernel, at, [hidden, hidden_c, grad_out, grad_out_c],
            [
                pl.BlockSpec((tokens, TILE), lambda i, at: (0, at[CORE_AT] * half_tiles + tile(i))),
                pl.BlockSpec((tokens, TILE), lambda i, at: (0, at[CORE_AT] * half_tiles + tile(i))),
                columns, columns,
            ],
            [shape((tokens + rest, pair))], [tile_spec], (lead + rest // TILE,), after=after,
        )[0]
        return away, send(away, X_LO)

    def width_kernel(at, turned_ref, *refs):
        total = 0.0
        for j in range(4):
            total = total + dot(turned_ref[:, j * slab:(j + 1) * slab], refs[j][...], 1, 1)
        for i in range(N_Y):
            refs[4 + i][...] = total[i * quarter:(i + 1) * quarter].astype(BF16)

    def scatter_sends(own, near, off, opposite):
        return own, near, send(opposite, Y_FIRST), send(off, Y_FIRST)

    def width_parts(k, after):
        forward = copy_of(at, weight_x[k], after=after)
        step = chunk // 2
        here = pl.BlockSpec((step, slab), lambda i, at: (2 * k + i, 0))
        there = pl.BlockSpec((step, slab), lambda i, at: (i, 0))
        return forward, lambda after: call(
            width_kernel, at, [turned, weight, weight_c, weight_x[k], send(forward, CORE)],
            [pl.BlockSpec(turned.shape, lambda i, at: (0, 0)), here, here, there, there],
            [shape((quarter, chunk))] * N_Y,
            [pl.BlockSpec((quarter, step), lambda i, at: (0, i))] * N_Y,
            (2,), after=after, vmem=16,
        )

    away, came_away = send_away([own_sum])
    forward, parts = width_parts(0, [away, hidden_x[0]])
    own, near, came_near, came_own = scatter_sends(*parts([forward]))
    near = add(at, [near, came_near])
    mine = [add(at, [own, came_own, send(near, Y_SECOND)])]
    forward, parts = width_parts(1, [mine[0], hidden_x[2]])
    own, near, came_near, came_own = scatter_sends(*parts([forward]))
    near = add(at, [near, came_near])
    mine.append(add(at, [own, came_own, send(near, Y_SECOND)]))
    beside = [send(m, X_HI) for m in mine]
    out_came = copy_of(at, came_away, tokens, after=[mine[1], hidden_x[1], hidden_x[3]])
    out_xc = send(out_came, CORE)

    def grad_kernel(at, sum_ref, a_low, a_high, b_low, b_high, out_x_ref, out_xc_ref, came_ref, result_ref):
        i = pl.program_id(0)

        def gathered(a_ref, b_ref):
            total = sum_ref[...] + dot(a_ref[...], out_x_ref[...], 0, 0)
            result_ref[...] = (total + dot(b_ref[...], out_xc_ref[...], 0, 0)).astype(BF16)

        bounds = [0, low // TILE, first_cut // TILE, n_tiles]
        for j, refs in enumerate(((a_low, b_low), (a_low, b_high), (a_high, b_high))):

            @pl.when((i >= bounds[j]) & (i < bounds[j + 1]))
            def _():
                gathered(*refs)

        @pl.when(i >= n_tiles)
        def _():
            result_ref[...] = (sum_ref[...] + came_ref[...].astype(F32)).astype(BF16)

    def cut_spec(start, size):
        return pl.BlockSpec(
            (tokens, TILE), lambda i, at: (0, jnp.clip(i - start // TILE, 0, size // TILE - 1))
        )

    all_out = pl.BlockSpec((tokens, pair), lambda i, at: (0, 0))
    own_half = call(
        grad_kernel, at, [own_sum, *hidden_x, came_away, out_xc, came_away],
        [
            tile_spec, *[cut_spec(start, size) for _, start, size in cuts], all_out, all_out,
            pl.BlockSpec((TILE, pair), lambda i, at: (lead + jnp.maximum(i - n_tiles, 0), 0)),
        ],
        [shape((half, pair))], [tile_spec], (half_tiles,), after=mine,
    )[0]
    other_half = send(own_half, CORE)

    num = tile_rows // BLK
    mine_rows = BLK // 2 // N_Y

    def left_kernel(at, own_low, own_high, other_low, other_high, *refs):
        outs, block, product = refs[:N_Y], refs[N_Y], refs[N_Y + 1]
        a = pl.program_id(0)
        for part, own_ref, other_ref in ((0, own_low, other_low), (1, own_high, other_high)):
            held = (2 * a + part) // half_tiles == at[CORE_AT]
            block[part * TILE:(part + 1) * TILE] = jnp.where(held, own_ref[...], other_ref[...])
        groups = block[...].reshape(16, 2, 16, pair)
        my_rows = jnp.where(at[CORE_AT] == 0, groups[:, 0], groups[:, 1]).reshape(BLK // 2, pair)
        product[...] = (dot(my_rows, block[...], 1, 1) / D).astype(BF16)
        for i, p in enumerate((Y, SECOND, FIRST, FAR)):
            outs[i][0] = product[pl.ds(pl.multiple_of(at[p] * mine_rows, mine_rows), mine_rows)]

    halves = [
        pl.BlockSpec((TILE, pair), lambda a, at, part=part: ((2 * a + part) % half_tiles, 0)) for part in (0, 1)
    ]
    left = left_parts = call(
        left_kernel, at, [own_half, own_half, other_half, other_half], halves + halves,
        [shape((num, mine_rows, BLK))] * N_Y,
        [pl.BlockSpec((1, mine_rows, BLK), lambda a, at: (a, 0, 0))] * N_Y,
        (num,), scratch=[pltpu.VMEM((BLK, pair), BF16), pltpu.VMEM((BLK // 2, BLK), BF16)],
        after=[own_half],
    )
    own, near, came_near, came_own = scatter_sends(*left)
    def go_round(total):
        near = send(total, Y_SECOND)
        off = send(total, Y_FIRST)
        return [total, near, off, send(near, Y_FIRST)]

    totals = [add(at, [mine[0], beside[0]], after=[came_near])]
    rounds = [go_round(totals[0])]
    def slab_kernel(at, own_ref, other_ref, result_ref, token_ref):
        token_ref[...] = jnp.zeros_like(token_ref)
        held = pl.program_id(0) == at[CORE_AT]
        result_ref[...] = jnp.where(held, own_ref[...], other_ref[...])

    slab_half = pl.BlockSpec((half, slab), lambda i, at: (0, at[CORE_AT]))
    grad_slab, slab_done = call(
        slab_kernel, at, [own_half, other_half], [slab_half] * 2, [shape(weight.shape), shape((8, 128), F32)],
        [pl.BlockSpec((half, slab), lambda i, at: (i, 0)), pl.BlockSpec((8, 128), lambda i, at: (0, 0))],
        (2,), after=totals,
    )


    def place_kernel(at, *refs):
        refs[-1][...] = jnp.zeros_like(refs[-1])
        for j in range(N_Y):

            @pl.when(pl.program_id(0) == j)
            def _():
                refs[-2][...] = refs[j][...]

    def place(k, given, grad_hidden, after):
        total = given[0]
        specs = [pl.BlockSpec(total.shape, lambda i, at: (0, 0))] * N_Y
        if k > 0:
            given, specs = given + [grad_hidden], specs + [ANY]
        return call(
            place_kernel, at, given, specs, [shape(hidden.shape), shape((8, 128), F32)],
            [
                pl.BlockSpec(total.shape, lambda i, at: (at[Y + i], k)),
                pl.BlockSpec((8, 128), lambda i, at: (0, 0)),
            ],
            (N_Y,), aliases={N_Y + 1: 0} if k > 0 else None, after=after,
        )

    upper = pair // 2

    def right_kernel(at, own_ref, other_ref, own_slab_ref, other_slab_ref, keep_ref, send_ref, total_ref):
        i = pl.program_id(0)
        value = dot(own_ref[...], own_slab_ref[...], 0, 0) + dot(other_ref[...], other_slab_ref[...], 0, 0)

        @pl.when(i == 0)
        def _():
            total_ref[...] = value

        @pl.when(i > 0)
        def _():
            total_ref[...] += value

        @pl.when(i == pl.num_programs(0) - 1)
        def _():
            here = at[Z_HIGH] * upper
            there = (1 - at[Z_HIGH]) * upper
            keep_ref[...] = total_ref[pl.ds(pl.multiple_of(here, upper), upper)] / FF
            send_ref[...] = (total_ref[pl.ds(pl.multiple_of(there, upper), upper)] / FF).astype(BF16)

    steps = 2
    rows_spec = pl.BlockSpec((half // steps, pair), lambda i, at: (i, 0))
    slab_spec = pl.BlockSpec((half // steps, slab), lambda i, at: (i, at[CORE_AT]))
    upper_spec = pl.BlockSpec((upper, slab), lambda i, at: (0, 0))

    stay, go = call(
        right_kernel, at, [own_half, other_half, own_half, other_half],
        [rows_spec, rows_spec, slab_spec, slab_spec],
        [shape((upper, slab), F32), shape((upper, slab))], [upper_spec] * 2, (steps,),
        scratch=[pltpu.VMEM((pair, slab), F32)], after=[slab_done],
    )

    blocks = (num * mine_rows, BLK)
    near = add(at, [near.reshape(blocks), came_near.reshape(blocks)], after=[stay, came_own, beside[1]])
    totals.append(add(at, [mine[1], beside[1]], after=[near, rounds[0][2]]))
    rounds.append(go_round(totals[1]))
    grad_hidden, placed = place(0, rounds[0], None, [totals[1]])
    def right_sum(stay, came, bit):
        rows = stay.shape[0] // 2

        def kernel(at_ref, stay_ref, came_ref, keep_ref, send_ref):
            total = stay_ref[...] + came_ref[...].astype(F32)
            here = at_ref[bit] == 0
            keep_ref[...] = jnp.where(here, total[:rows], total[rows:])
            send_ref[...] = jnp.where(here, total[rows:], total[:rows]).astype(BF16)

        whole = pl.BlockSpec(stay.shape, lambda i, at: (0, 0))
        half_of = pl.BlockSpec((rows, slab), lambda i, at: (0, 0))
        return call(
            kernel, at, [stay, came], [whole] * 2, [shape((rows, slab), F32), shape((rows, slab))], [half_of] * 2
        )

    right_steps = []
    for i, bit in enumerate(bits):
        came_z = lax.ppermute(go, "col", [(j, j ^ bit) for j in range(cols)])
        if i < len(bits) - 1:
            stay, go = right_sum(stay, came_z, Z_HIGH + 1 + i)
            right_steps.append(stay)

    near = near.reshape(own.shape)
    def left_sum(parts, groups, bit, after=()):
        def kernel(at_ref, *refs):
            total = refs[0][...].astype(F32)
            for ref in refs[1:-2]:
                total = total + ref[...].astype(F32)
            total = total.reshape((num * groups // 2, 2, 16, BLK))
            stays = at_ref[bit] == 0
            rows = (num, groups * 8, BLK)
            refs[-2][...] = jnp.where(stays, total[:, 0], total[:, 1]).reshape(rows)
            refs[-1][...] = jnp.where(stays, total[:, 1], total[:, 0]).reshape(rows).astype(BF16)

        whole = pl.BlockSpec((num, groups * 16, BLK), lambda a, at: (0, 0, 0))
        half_of = pl.BlockSpec((num, groups * 8, BLK), lambda a, at: (0, 0, 0))
        return call(
            kernel, at, parts, [whole] * len(parts),
            [shape((num, groups * 8, BLK), F32), shape((num, groups * 8, BLK))], [half_of] * 2, after=after,
        )

    stays, goes = left_sum([own, came_own, send(near, Y_SECOND)], 4, X_LO_AT, right_steps[:1])
    stays, goes = left_sum([stays, send(goes, X_LO)], 2, X_HI_AT, [*right_steps[1:], rounds[1][2]])
    left_stats = stays + send(goes, X_HI).astype(F32)

    def last_kernel(at, mine_ref, came_ref, result_ref):
        result_ref[...] = mine_ref[...] + came_ref[...].astype(F32)

    spec = pl.BlockSpec(stay.shape, lambda i, at: (0, 0))
    right_stats = call(
        last_kernel, at, [stay, came_z], [spec] * 2, [shape(stay.shape, F32)], [spec], after=[placed]
    )[0].T

    grad_hidden, _ = place(1, rounds[1], grad_hidden, [left_stats, right_stats])
    return grad_hidden, grad_slab, left_stats, right_stats


def solution(mesh):
    return jax.shard_map(
        body,
        mesh=mesh,
        in_specs=(P("rep", "col"), P("rep", "row"), P("col", ("row", "rep"))),
        out_specs=(
            P("rep", "col"),
            P("col", ("row", "rep")),
            P("col", ("row", "rep"), None),
            P(("row", "rep"), "col"),
        ),
        check_vma=False,
    )
```

```python
import jax
import jax.numpy as jnp
from jax import lax
from jax.experimental import pallas as pl
from jax.experimental.pallas import tpu as pltpu
from jax.sharding import PartitionSpec as P

D = 8192
FF = 28672
BLK = 512
N_Y = 4
A_CHUNKS = 2
GATHERED_ROWS = 1280
TILE = 256
F32 = jnp.float32
BF16 = jnp.bfloat16

Y, SECOND, FIRST, FAR, SLAB, SLAB_C, SLAB_X, SLAB_XC, CORE_AT, X_LO_AT, X_HI_AT, Z_HIGH = range(12)


def plane_perm(move):
    pairs = []
    for at in range(32):
        y, x_hi, x_lo, core = at // 8, at // 4 % 2, at // 2 % 2, at % 2
        y, x_hi, x_lo, core = move(y, x_hi, x_lo, core)
        pairs.append((at, y * 8 + x_hi * 4 + x_lo * 2 + core))
    return pairs


CORE = plane_perm(lambda y, h, l, c: (y, h, l, 1 - c))
X_LO = plane_perm(lambda y, h, l, c: (y, h, 1 - l, c))
X_HI = plane_perm(lambda y, h, l, c: (y, 1 - h, l, c))
X_OUT = plane_perm(lambda y, h, l, c: (y, 1 - h, 1 - l, c))
X_OUT_CORE = plane_perm(lambda y, h, l, c: (y, 1 - h, 1 - l, 1 - c))
Y_FIRST = plane_perm(lambda y, h, l, c: (y ^ (3 if c else 1), h, l, c))
Y_SECOND = plane_perm(lambda y, h, l, c: (y ^ (1 if c else 3), h, l, c))


def send(x, perm):
    return lax.ppermute(x, ("row", "rep"), perm)


def shape(dims, dtype=BF16):
    return jax.ShapeDtypeStruct(dims, dtype)


ANY = pl.BlockSpec(memory_space=pl.ANY)


def call(kernel, at, arrays, in_specs, outs, out_specs, grid=(1,), scratch=(), after=(), aliases=None, vmem=10):
    n, m = len(arrays), len(after)

    def run(at_ref, *refs):
        kernel(at_ref, *refs[:n], *refs[n + m:])

    return pl.pallas_call(
        run,
        grid_spec=pltpu.PrefetchScalarGridSpec(
            num_scalar_prefetch=1,
            grid=grid,
            in_specs=list(in_specs) + [ANY] * m,
            out_specs=list(out_specs),
            scratch_shapes=list(scratch),
        ),
        out_shape=list(outs),
        input_output_aliases=aliases or {},
        compiler_params=pltpu.CompilerParams(vmem_limit_bytes=vmem * 2**20),
        cost_estimate=pl.CostEstimate(flops=1, bytes_accessed=1, transcendentals=0),
    )(at, *arrays, *after)


def copies(at, arrays, outs, plan, count, after=(), vmem=16):
    n = len(arrays)

    def kernel(at_ref, *refs):
        sems = refs[-1]
        moves = [
            pltpu.make_async_copy(src, dst, sems.at[i])
            for i, (src, dst) in enumerate(plan(at_ref, refs[:n], refs[n:-1]))
        ]
        for move in moves:
            move.start()
        for move in moves:
            move.wait()

    return call(
        kernel, at, arrays, [pl.BlockSpec(memory_space=pltpu.HBM)] * n, outs,
        [pl.BlockSpec(out.shape, lambda i, at: (0, 0)) for out in outs],
        scratch=[pltpu.SemaphoreType.DMA((count,))], after=after, vmem=vmem,
    )


def add(at, arrays, after=()):
    rows, width = arrays[0].shape
    spec = pl.BlockSpec((rows, width // 2), lambda i, at: (0, i))

    def kernel(at_ref, *refs):
        total = refs[0][...].astype(F32)
        for ref in refs[1:-1]:
            total = total + ref[...].astype(F32)
        refs[-1][...] = total.astype(BF16)

    return call(kernel, at, arrays, [spec] * len(arrays), [shape((rows, width))], [spec], (2,), after=after)[0]


def copy_of(at, x, rows=None, after=()):
    rows = rows or x.shape[0]
    spec = pl.BlockSpec((rows // 2, x.shape[1]), lambda i, at: (i, 0))

    def kernel(at_ref, x_ref, out_ref):
        out_ref[...] = x_ref[...]

    return call(kernel, at, [x], [spec], [shape((rows, x.shape[1]))], [spec], (2,), after=after)[0]


def dot(a, b, over_a, over_b):
    return lax.dot_general(a, b, (((over_a,), (over_b,)), ((), ())), preferred_element_type=F32)


def part_rows(x, at, rows):
    return lax.dynamic_slice_in_dim(x, at * rows, rows, 0)


def piece(x, at, axis):
    return lax.dynamic_index_in_dim(x, at, axis, keepdims=False)


def body(hidden, grad_out, weight):
    row, rep = lax.axis_index("row"), lax.axis_index("rep")
    y, x_hi = row // 2, row % 2
    x_lo, core = rep // 2, rep % 2
    first = y ^ (1 + 2 * core)
    second = y ^ (3 - 2 * core)
    z = lax.axis_index("col")
    cols = lax.axis_size("col")
    bits = [1 << i for i in reversed(range(cols.bit_length() - 1))]
    at = jnp.stack([y, second, first, y ^ 2, rep, rep ^ 1, rep ^ 2, rep ^ 3, core, x_lo, x_hi, *[z // bit % 2 for bit in bits]]).astype(jnp.int32)
    tokens, tile_rows = hidden.shape
    slab = weight.shape[1]
    half = tile_rows // 2
    pair = 2 * slab
    n = GATHERED_ROWS
    rest = half - n
    chunk = tile_rows // A_CHUNKS
    quarter = tokens // N_Y
    half_tiles, n_tiles, chunk_tiles = half // TILE, n // TILE, chunk // TILE

    hidden_c, grad_out_c, weight_c = (send(x, CORE) for x in (hidden, grad_out, weight))
    weight_x = [send(weight[:chunk], X_LO)]
    first_cut, low = (n_tiles - 1) * TILE, (n_tiles + 1) // 2 * TILE
    cuts = [(0, 0, first_cut), (0, first_cut, n - first_cut), (1, 0, low), (1, low, n - low)]

    def hidden_moves(at, hidden_ref, out, cut):
        other, start, size = cut
        start = pl.multiple_of((1 - at[CORE_AT] if other else at[CORE_AT]) * half, TILE) + start
        step = tokens // 4
        return [
            (hidden_ref.at[pl.ds(j * step, step), pl.ds(start, size)], out.at[pl.ds(j * step, step)])
            for j in range(4)
        ]

    cut_shapes = [shape((tokens, size)) for _, _, size in cuts]
    hidden_sent = copies(
        at, [hidden], cut_shapes[:1], lambda at, ins, outs: hidden_moves(at, ins[0], outs[0], cuts[0]), 4
    )
    hidden_x = [send(hidden_sent[0], X_OUT)]
    *hidden_late, weight_late = copies(
        at, [hidden, weight], cut_shapes[1:] + [shape((chunk, slab))],
        lambda at, ins, outs: [
            *hidden_moves(at, ins[0], outs[0], cuts[1]), *hidden_moves(at, ins[0], outs[1], cuts[2]),
            *hidden_moves(at, ins[0], outs[2], cuts[3]), (ins[1].at[pl.ds(chunk, chunk)], outs[3]),
        ], 13, after=hidden_sent,
    )
    weight_x.append(send(weight_late, X_LO))
    hidden_x += [send(h, p) for h, p in zip(hidden_late, (X_OUT, X_OUT_CORE, X_OUT_CORE))]

    def turn_plan(at, ins, outs):
        moves = []
        for i, p in enumerate((Y, SECOND, FIRST, FAR)):
            for j, s in enumerate((SLAB, SLAB_C, SLAB_X, SLAB_XC)):
                src = ins[0].at[
                    pl.ds(pl.multiple_of(at[p] * quarter, quarter), quarter),
                    pl.ds(pl.multiple_of(at[s] * slab, slab), slab),
                ]
                moves.append((src, outs[0].at[pl.ds(i * quarter, quarter), pl.ds(j * slab, slab)]))
        return moves

    turned = copies(at, [grad_out], [shape(grad_out.shape)], turn_plan, 16, after=[weight_late])[0]

    def sum_kernel(at, hidden_ref, hidden_c_ref, out_ref, out_c_ref, result_ref):
        result_ref[...] = dot(hidden_ref[...], out_ref[...], 0, 0) + dot(hidden_c_ref[...], out_c_ref[...], 0, 0)

    tile_spec = pl.BlockSpec((TILE, pair), lambda i, at: (i, 0))
    own_columns = pl.BlockSpec((tokens, pair), lambda i, at: (0, at[X_LO_AT]))
    own_sum = call(
        sum_kernel, at, [hidden, hidden_c, grad_out, grad_out_c],
        [
            pl.BlockSpec((tokens, TILE), lambda i, at: (0, at[CORE_AT] * half_tiles + i)),
            pl.BlockSpec((tokens, TILE), lambda i, at: (0, at[CORE_AT] * half_tiles + i)),
            own_columns, own_columns,
        ],
        [shape((half, pair), F32)], [tile_spec], (half_tiles,), after=[turned],
    )[0]

    lead = tokens // TILE

    def away_kernel(at, hidden_ref, hidden_c_ref, out_ref, out_c_ref, result_ref):
        i = pl.program_id(0)

        @pl.when(i < lead)
        def _():
            result_ref[...] = out_ref[pl.ds(pl.multiple_of(i * TILE, TILE), TILE)]

        @pl.when(i >= lead)
        def _():
            total = dot(hidden_ref[...], out_ref[...], 0, 0) + dot(hidden_c_ref[...], out_c_ref[...], 0, 0)
            result_ref[...] = total.astype(BF16)

    def send_away(after):
        columns = pl.BlockSpec((tokens, pair), lambda i, at: (0, 1 - at[X_LO_AT]))
        tile = lambda i: n_tiles + jnp.maximum(i - lead, 0)
        away = call(
            away_kernel, at, [hidden, hidden_c, grad_out, grad_out_c],
            [
                pl.BlockSpec((tokens, TILE), lambda i, at: (0, at[CORE_AT] * half_tiles + tile(i))),
                pl.BlockSpec((tokens, TILE), lambda i, at: (0, at[CORE_AT] * half_tiles + tile(i))),
                columns, columns,
            ],
            [shape((tokens + rest, pair))], [tile_spec], (lead + rest // TILE,), after=after,
        )[0]
        return away, send(away, X_LO)

    def width_kernel(at, turned_ref, *refs):
        total = 0.0
        for j in range(4):
            total = total + dot(turned_ref[:, j * slab:(j + 1) * slab], refs[j][...], 1, 1)
        for i in range(N_Y):
            refs[4 + i][...] = total[i * quarter:(i + 1) * quarter].astype(BF16)

    def scatter_sends(own, near, off, opposite):
        return own, near, send(opposite, Y_FIRST), send(off, Y_FIRST)

    def width_parts(k, after):
        forward = copy_of(at, weight_x[k], after=after)
        step = chunk // 2
        here = pl.BlockSpec((step, slab), lambda i, at: (2 * k + i, 0))
        there = pl.BlockSpec((step, slab), lambda i, at: (i, 0))
        return forward, lambda after: call(
            width_kernel, at, [turned, weight, weight_c, weight_x[k], send(forward, CORE)],
            [pl.BlockSpec(turned.shape, lambda i, at: (0, 0)), here, here, there, there],
            [shape((quarter, chunk))] * N_Y,
            [pl.BlockSpec((quarter, step), lambda i, at: (0, i))] * N_Y,
            (2,), after=after, vmem=16,
        )

    away, came_away = send_away([own_sum])
    forward, parts = width_parts(0, [away, hidden_x[0]])
    own, near, came_near, came_own = scatter_sends(*parts([forward]))
    near = add(at, [near, came_near])
    mine = [add(at, [own, came_own, send(near, Y_SECOND)])]
    forward, parts = width_parts(1, [mine[0], hidden_x[2]])
    own, near, came_near, came_own = scatter_sends(*parts([forward]))
    near = add(at, [near, came_near])
    mine.append(add(at, [own, came_own, send(near, Y_SECOND)]))
    beside = [send(m, X_HI) for m in mine]
    out_came = copy_of(at, came_away, tokens, after=[mine[1], hidden_x[1], hidden_x[3]])
    out_xc = send(out_came, CORE)

    def grad_kernel(at, sum_ref, a_low, a_high, b_low, b_high, out_x_ref, out_xc_ref, came_ref, result_ref):
        i = pl.program_id(0)

        def gathered(a_ref, b_ref):
            total = sum_ref[...] + dot(a_ref[...], out_x_ref[...], 0, 0)
            result_ref[...] = (total + dot(b_ref[...], out_xc_ref[...], 0, 0)).astype(BF16)

        bounds = [0, low // TILE, first_cut // TILE, n_tiles]
        for j, refs in enumerate(((a_low, b_low), (a_low, b_high), (a_high, b_high))):

            @pl.when((i >= bounds[j]) & (i < bounds[j + 1]))
            def _():
                gathered(*refs)

        @pl.when(i >= n_tiles)
        def _():
            result_ref[...] = (sum_ref[...] + came_ref[...].astype(F32)).astype(BF16)

    def cut_spec(start, size):
        return pl.BlockSpec(
            (tokens, TILE), lambda i, at: (0, jnp.clip(i - start // TILE, 0, size // TILE - 1))
        )

    all_out = pl.BlockSpec((tokens, pair), lambda i, at: (0, 0))
    own_half = call(
        grad_kernel, at, [own_sum, *hidden_x, came_away, out_xc, came_away],
        [
            tile_spec, *[cut_spec(start, size) for _, start, size in cuts], all_out, all_out,
            pl.BlockSpec((TILE, pair), lambda i, at: (lead + jnp.maximum(i - n_tiles, 0), 0)),
        ],
        [shape((half, pair))], [tile_spec], (half_tiles,), after=mine,
    )[0]
    other_half = send(own_half, CORE)

    num = tile_rows // BLK
    mine_rows = BLK // 2 // N_Y

    def left_kernel(at, own_low, own_high, other_low, other_high, *refs):
        outs, block, product = refs[:N_Y], refs[N_Y], refs[N_Y + 1]
        a = pl.program_id(0)
        for part, own_ref, other_ref in ((0, own_low, other_low), (1, own_high, other_high)):
            held = (2 * a + part) // half_tiles == at[CORE_AT]
            block[part * TILE:(part + 1) * TILE] = jnp.where(held, own_ref[...], other_ref[...])
        groups = block[...].reshape(16, 2, 16, pair)
        my_rows = jnp.where(at[CORE_AT] == 0, groups[:, 0], groups[:, 1]).reshape(BLK // 2, pair)
        product[...] = (dot(my_rows, block[...], 1, 1) / D).astype(BF16)
        for i, p in enumerate((Y, SECOND, FIRST, FAR)):
            outs[i][0] = product[pl.ds(pl.multiple_of(at[p] * mine_rows, mine_rows), mine_rows)]

    halves = [
        pl.BlockSpec((TILE, pair), lambda a, at, part=part: ((2 * a + part) % half_tiles, 0)) for part in (0, 1)
    ]
    left = left_parts = call(
        left_kernel, at, [own_half, own_half, other_half, other_half], halves + halves,
        [shape((num, mine_rows, BLK))] * N_Y,
        [pl.BlockSpec((1, mine_rows, BLK), lambda a, at: (a, 0, 0))] * N_Y,
        (num,), scratch=[pltpu.VMEM((BLK, pair), BF16), pltpu.VMEM((BLK // 2, BLK), BF16)],
        after=[own_half],
    )
    own, near, came_near, came_own = scatter_sends(*left)
    def go_round(total):
        near = send(total, Y_SECOND)
        return [total, near, send(total, Y_FIRST)]

    totals = [add(at, [mine[0], beside[0]], after=[came_near])]
    rounds = [go_round(totals[0])]
    rounds[0].append(send(rounds[0][1], Y_FIRST))
    def slab_kernel(at, own_ref, other_ref, result_ref, token_ref):
        token_ref[...] = jnp.zeros_like(token_ref)
        held = pl.program_id(0) == at[CORE_AT]
        result_ref[...] = jnp.where(held, own_ref[...], other_ref[...])

    slab_half = pl.BlockSpec((half, slab), lambda i, at: (0, at[CORE_AT]))
    grad_slab, slab_done = call(
        slab_kernel, at, [own_half, other_half], [slab_half] * 2, [shape(weight.shape), shape((8, 128), F32)],
        [pl.BlockSpec((half, slab), lambda i, at: (i, 0)), pl.BlockSpec((8, 128), lambda i, at: (0, 0))],
        (2,), after=totals,
    )


    def place_kernel(at, *refs):
        refs[-1][...] = jnp.zeros_like(refs[-1])
        for j in range(N_Y):

            @pl.when(pl.program_id(0) == j)
            def _():
                refs[-2][...] = refs[j][...]

    def place(k, given, grad_hidden, after):
        total = given[0]
        specs = [pl.BlockSpec(total.shape, lambda i, at: (0, 0))] * N_Y
        if k > 0:
            given, specs = given + [grad_hidden], specs + [ANY]
        return call(
            place_kernel, at, given, specs, [shape(hidden.shape), shape((8, 128), F32)],
            [
                pl.BlockSpec(total.shape, lambda i, at: (at[Y + i], k)),
                pl.BlockSpec((8, 128), lambda i, at: (0, 0)),
            ],
            (N_Y,), aliases={N_Y + 1: 0} if k > 0 else None, after=after,
        )

    upper = pair // 2

    def right_kernel(at, own_ref, other_ref, own_slab_ref, other_slab_ref, keep_ref, send_ref, total_ref):
        i = pl.program_id(0)
        value = dot(own_ref[...], own_slab_ref[...], 0, 0) + dot(other_ref[...], other_slab_ref[...], 0, 0)

        @pl.when(i == 0)
        def _():
            total_ref[...] = value

        @pl.when(i > 0)
        def _():
            total_ref[...] += value

        @pl.when(i == pl.num_programs(0) - 1)
        def _():
            here = at[Z_HIGH] * upper
            there = (1 - at[Z_HIGH]) * upper
            keep_ref[...] = total_ref[pl.ds(pl.multiple_of(here, upper), upper)] / FF
            send_ref[...] = (total_ref[pl.ds(pl.multiple_of(there, upper), upper)] / FF).astype(BF16)

    steps = 2
    rows_spec = pl.BlockSpec((half // steps, pair), lambda i, at: (i, 0))
    slab_spec = pl.BlockSpec((half // steps, slab), lambda i, at: (i, at[CORE_AT]))
    upper_spec = pl.BlockSpec((upper, slab), lambda i, at: (0, 0))

    stay, go = call(
        right_kernel, at, [own_half, other_half, own_half, other_half],
        [rows_spec, rows_spec, slab_spec, slab_spec],
        [shape((upper, slab), F32), shape((upper, slab))], [upper_spec] * 2, (steps,),
        scratch=[pltpu.VMEM((pair, slab), F32)], after=[slab_done],
    )

    blocks = (num * mine_rows, BLK)
    near = add(at, [near.reshape(blocks), came_near.reshape(blocks)], after=[stay, came_own, beside[1]])
    totals.append(add(at, [mine[1], beside[1]], after=[near, rounds[0][2]]))
    rounds.append(go_round(totals[1]))
    grad_hidden, placed = place(0, rounds[0], None, [near])

    def right_sum(stay, came, bit, after):
        rows = stay.shape[0] // 2

        def kernel(at_ref, stay_ref, came_ref, keep_ref, send_ref):
            total = stay_ref[...] + came_ref[...].astype(F32)
            here = at_ref[bit] == 0
            keep_ref[...] = jnp.where(here, total[:rows], total[rows:])
            send_ref[...] = jnp.where(here, total[rows:], total[:rows]).astype(BF16)

        whole = pl.BlockSpec(stay.shape, lambda i, at: (0, 0))
        half_of = pl.BlockSpec((rows, slab), lambda i, at: (0, 0))
        return call(
            kernel, at, [stay, came], [whole] * 2, [shape((rows, slab), F32), shape((rows, slab))], [half_of] * 2,
            after=after,
        )

    right_steps = []
    for i, bit in enumerate(bits):
        came_z = lax.ppermute(go, "col", [(j, j ^ bit) for j in range(cols)])
        if i < len(bits) - 1:
            stay, go = right_sum(stay, came_z, Z_HIGH + 1 + i, [placed] if i else [])
            right_steps.append(stay)

    near = near.reshape(own.shape)
    def left_sum(parts, groups, bit, after=()):
        def kernel(at_ref, *refs):
            total = refs[0][...].astype(F32)
            for ref in refs[1:-2]:
                total = total + ref[...].astype(F32)
            total = total.reshape((num * groups // 2, 2, 16, BLK))
            stays = at_ref[bit] == 0
            rows = (num, groups * 8, BLK)
            refs[-2][...] = jnp.where(stays, total[:, 0], total[:, 1]).reshape(rows)
            refs[-1][...] = jnp.where(stays, total[:, 1], total[:, 0]).reshape(rows).astype(BF16)

        whole = pl.BlockSpec((num, groups * 16, BLK), lambda a, at: (0, 0, 0))
        half_of = pl.BlockSpec((num, groups * 8, BLK), lambda a, at: (0, 0, 0))
        return call(
            kernel, at, parts, [whole] * len(parts),
            [shape((num, groups * 8, BLK), F32), shape((num, groups * 8, BLK))], [half_of] * 2, after=after,
        )

    stays, goes = left_sum([own, came_own, send(near, Y_SECOND)], 4, X_LO_AT, right_steps[:1])
    passed = copy_of(at, rounds[1][1], after=[goes])
    stays, goes = left_sum([stays, send(goes, X_LO)], 2, X_HI_AT, [*right_steps[1:], rounds[1][2]])
    came = send(goes, X_HI)

    rounds[1].append(send(passed, Y_FIRST))
    grad_hidden, placed = place(1, rounds[1], grad_hidden, [goes, right_steps[-1]])

    def last_kernel(at, mine_ref, came_ref, result_ref):
        result_ref[...] = mine_ref[...] + came_ref[...].astype(F32)

    spec = pl.BlockSpec(stay.shape, lambda i, at: (0, 0))
    right_stats = call(
        last_kernel, at, [stay, came_z], [spec] * 2, [shape(stay.shape, F32)], [spec], after=[placed]
    )[0].T
    spec = pl.BlockSpec(stays.shape, lambda i, at: (0, 0, 0))
    left_stats = call(last_kernel, at, [stays, came], [spec] * 2, [shape(stays.shape, F32)], [spec], after=[placed])[0]

    return grad_hidden, grad_slab, left_stats, right_stats


def solution(mesh):
    return jax.shard_map(
        body,
        mesh=mesh,
        in_specs=(P("rep", "col"), P("rep", "row"), P("col", ("row", "rep"))),
        out_specs=(
            P("rep", "col"),
            P("col", ("row", "rep")),
            P("col", ("row", "rep"), None),
            P(("row", "rep"), "col"),
        ),
        check_vma=False,
    )
```
